32 devices in a mesh: dp: 8 (over y, x, core), graph: 4 (over z).
Axes of the slice: x: 2, y: 2, z: 4, core: 2. Of those that a mesh axis runs over, the one named last changes fastest.
Arguments:
- nodes: bfloat16 [8, 64, 6272], P('dp', 'graph'), may hold values from -6 to 6
- sources: int32 [8, 2048], P('dp', 'graph'), may hold values from 0 to 63
- targets: int32 [8, 2048], P('dp', 'graph'), may hold values from 0 to 63
- edge_counts: int32 [8, 4], P('dp', 'graph'), may hold values from 128 to 512, as said below
- wigner: bfloat16 [8, 29, 49, 2048], P('dp', None, None, 'graph'), as said below
- radial: bfloat16 [8, 2048, 128], P('dp', 'graph'), may hold values from 0.5 to 1.5
- cotangent: bfloat16 [8, 64, 6272], P('dp', 'graph'), may hold values from -6 to 6
- w_zero: bfloat16 [896, 896], replicated, may hold values from -0.1875 to 0.1875
- w_one: bfloat16 [2, 768, 768], replicated, may hold values from -0.15625 to 0.15625
- w_two: bfloat16 [2, 640, 640], replicated, may hold values from -0.15625 to 0.15625
- w_gate: bfloat16 [128, 128], replicated, may hold values from -0.5 to 0.5
Outputs:
- aggregated: bfloat16 [8, 64, 6272], P('dp', 'graph')
- grad_nodes: bfloat16 [8, 64, 6272], P('dp', 'graph')
- grad_zero: float32 [896, 896], replicated
- grad_one: float32 [2, 768, 768], replicated
- grad_two: float32 [2, 640, 640], replicated
- grad_gate: float32 [128, 128], replicated
The draws below stay inside these ranges and needn't reach their ends.
Inputs may be any that keep to these rules, and one draw needn't show every extreme that they name: `edge_counts`: one shard of each batch holds 512 live slots; live slots come first in each shard. `wigner`: for each edge, entry (k, j) is zero unless kept coefficient k and coefficient j have the same degree.
All inputs are finite; a program needn't handle non-finite values.
Results may differ from the reference program's by a relative error of at most 0.013.
Values may be sent and summed in bfloat16 or wider, within the bound.
No kernel may reach another device: no remote copies, remote signals or barrier semaphores. Data moves between devices by JAX's collectives and lax.ppermute only.
A program may use at most 128 MiB of HBM per device.

```python
import jax
import jax.numpy as jnp
import numpy as np
from jax import lax

C = 128
LMAX = 6
COEF = 49
KEPT = 29
EDGE_DEV = 512
NODES = 64
EDGES = 2048
BATCHES = 8
N_GRAPH = 4


def draw_edge_counts(key, part):
    first_key, second_key = jax.random.split(key)
    counts = jax.random.randint(first_key, (BATCHES, N_GRAPH), EDGE_DEV // 4, EDGE_DEV + 1)
    fullest = jax.random.randint(second_key, (BATCHES, 1), 0, N_GRAPH)
    columns = jnp.arange(N_GRAPH, dtype=jnp.int32)[None, :]
    return jnp.where(columns == fullest, EDGE_DEV, counts).astype(jnp.int32)


def draw_wigner(key, part):
    kept_degrees = np.array(list(range(LMAX + 1)) + list(range(1, LMAX + 1)) * 2 + list(range(2, LMAX + 1)) * 2)
    full_degrees = np.array([degree for degree in range(LMAX + 1) for order in range(2 * degree + 1)])
    matching = (kept_degrees[:, None] == full_degrees[None, :]).astype(np.float32)
    scaling = matching / np.sqrt(2.0 * full_degrees[None, :] + 1.0).astype(np.float32)
    values = jax.random.normal(key, (BATCHES, KEPT, COEF, EDGES), jnp.float32)
    return (values * jnp.asarray(scaling)[None, :, :, None]).astype(jnp.bfloat16)


def touch_ends(values, rng, low, high):
    index_at = [jax.random.randint(jax.random.fold_in(rng, axis), (), 0, length) for axis, length in enumerate(values.shape)]
    main_axis = values.shape.index(max(values.shape))
    next_to = index_at[:main_axis] + [(index_at[main_axis] + 1) % values.shape[main_axis]] + index_at[main_axis + 1:]
    return values.at[tuple(index_at)].set(low).at[tuple(next_to)].set(high)


def block_scale(rng, shape, cuts, low, largest):
    def one(dim, blocks):
        steps = jax.random.uniform(jax.random.fold_in(jax.random.fold_in(rng, 6), dim), (blocks,), jnp.float32, low / len(cuts), largest / len(cuts))
        return jnp.repeat(jnp.exp(steps), shape[dim] // blocks).reshape((-1,) + (1,) * (len(shape) - dim - 1))

    gain = one(*cuts[0])
    for cut in cuts[1:]:
        gain = gain * one(*cut)
    return gain


def noise(stream_key, dims, scale, bound, cuts=(), kind=jnp.bfloat16):
    result = scale * jax.random.normal(stream_key, dims, jnp.float32)
    if cuts:
        result = result * block_scale(stream_key, dims, cuts, -0.22, 0.18)
    return jnp.clip(result, -bound, bound).astype(kind)


def setup_inputs(seed: int = 0) -> dict:
    arg_keys = jax.random.split(jax.random.key(seed), 12)
    nodes = noise(arg_keys[0], (BATCHES, NODES, COEF * C), 1.0, 6.0, ((0, 8), (1, 4)))
    sources = touch_ends(jax.random.randint(arg_keys[1], (BATCHES, EDGES), 0, NODES), jax.random.fold_in(arg_keys[1], 1), 0, NODES - 1).astype(jnp.int32)
    targets = touch_ends(jax.random.randint(arg_keys[2], (BATCHES, EDGES), 0, NODES), jax.random.fold_in(arg_keys[2], 1), 0, NODES - 1).astype(jnp.int32)
    edge_counts = draw_edge_counts(jax.random.fold_in(arg_keys[11], 71), 0)
    wigner = draw_wigner(jax.random.fold_in(arg_keys[11], 71), 0)
    radial = jnp.clip(0.5 + 1.0 * jax.random.uniform(arg_keys[5], (BATCHES, EDGES, C), jnp.float32) ** block_scale(arg_keys[5], (BATCHES, EDGES, C), ((0, 8), (1, 4)), -0.2, 0.2), 0.5, 1.5).astype(jnp.bfloat16)
    cotangent = noise(arg_keys[6], (BATCHES, NODES, COEF * C), 1.0, 6.0, ((0, 8), (1, 4)))
    w_zero = noise(arg_keys[7], (7 * C, 7 * C), (7 * C) ** -0.5, 0.1875)
    w_one = noise(arg_keys[8], (2, 6 * C, 6 * C), (12 * C) ** -0.5, 0.15625)
    w_two = noise(arg_keys[9], (2, 5 * C, 5 * C), (10 * C) ** -0.5, 0.15625)
    w_gate = noise(arg_keys[10], (C, C), C ** -0.5, 0.5)
    return {"nodes": nodes, "sources": sources, "targets": targets, "edge_counts": edge_counts, "wigner": wigner, "radial": radial, "cotangent": cotangent, "w_zero": w_zero, "w_one": w_one, "w_two": w_two, "w_gate": w_gate}


def product(left, right):
    return jnp.dot(left, right, preferred_element_type=jnp.float32)


def product_left(left, right):
    return lax.dot_general(left, right, (((0,), (0,)), ((), ())), preferred_element_type=jnp.float32)


def product_right(left, right):
    return lax.dot_general(left, right, (((1,), (1,)), ((), ())), preferred_element_type=jnp.float32)


def split_kept(values):
    rows = values.shape[0]
    bounds = ((0, 7), (7, 13), (13, 19), (19, 24), (24, 29))
    return tuple(values[:, lower:upper, :].reshape(rows, -1) for lower, upper in bounds)


def edge_forward(gathered, rotation, radial_rows, valid, w_zero, w_one, w_two, w_gate):
    rows = gathered.shape[0]
    width = w_gate.shape[0]
    turned = jnp.einsum("kje,ejc->ekc", rotation.astype(jnp.float32), gathered.astype(jnp.float32))
    rotated = (turned * radial_rows.astype(jnp.float32)[:, None, :]).astype(jnp.bfloat16)
    zero_part, plus_one, minus_one, plus_two, minus_two = split_kept(rotated)
    mixed = jnp.concatenate([
        product(zero_part, w_zero),
        product(plus_one, w_one[0]) - product(minus_one, w_one[1]),
        product(plus_one, w_one[1]) + product(minus_one, w_one[0]),
        product(plus_two, w_two[0]) - product(minus_two, w_two[1]),
        product(plus_two, w_two[1]) + product(minus_two, w_two[0])], axis=1).reshape(rows, -1, width)
    scalar = mixed[:, 0, :]
    scalar_low = scalar.astype(jnp.bfloat16)
    gate = jax.nn.sigmoid(product(scalar_low, w_gate))
    message = jnp.concatenate([jax.nn.silu(scalar)[:, None, :], mixed[:, 1:, :] * gate[:, None, :]], axis=1)
    message = (message * valid[:, None, None].astype(jnp.float32)).astype(jnp.bfloat16)
    back = jnp.einsum("kje,ekc->ejc", rotation.astype(jnp.float32), message.astype(jnp.float32)).astype(jnp.bfloat16)
    return back, (rotated, mixed, scalar_low, gate)


def edge_backward(upstream, rotation, radial_rows, saved, w_zero, w_one, w_two, w_gate):
    rotated, mixed, scalar_low, gate = saved
    rows = upstream.shape[0]
    width = w_gate.shape[0]
    incoming = jnp.einsum("kje,ejc->ekc", rotation.astype(jnp.float32), upstream.astype(jnp.float32))
    scalar = mixed[:, 0, :]
    sigmoid_value = jax.nn.sigmoid(scalar)
    direct = incoming[:, 0, :] * sigmoid_value * (1.0 + scalar * (1.0 - sigmoid_value))
    gate_low = (jnp.sum(incoming[:, 1:, :] * mixed[:, 1:, :], axis=1) * gate * (1.0 - gate)).astype(jnp.bfloat16)
    head = direct + product_right(gate_low, w_gate)
    mixed_grad = jnp.concatenate([head[:, None, :], incoming[:, 1:, :] * gate[:, None, :]], axis=1).astype(jnp.bfloat16)
    zero_grad, plus_one_grad, minus_one_grad, plus_two_grad, minus_two_grad = split_kept(mixed_grad)
    zero_part, plus_one, minus_one, plus_two, minus_two = split_kept(rotated)
    grad_zero = product_left(zero_part, zero_grad)
    grad_one = jnp.stack([
        product_left(plus_one, plus_one_grad) + product_left(minus_one, minus_one_grad),
        product_left(plus_one, minus_one_grad) - product_left(minus_one, plus_one_grad)])
    grad_two = jnp.stack([
        product_left(plus_two, plus_two_grad) + product_left(minus_two, minus_two_grad),
        product_left(plus_two, minus_two_grad) - product_left(minus_two, plus_two_grad)])
    grad_gate = product_left(scalar_low, gate_low)
    backward_parts = jnp.concatenate([
        product_right(zero_grad, w_zero),
        product_right(plus_one_grad, w_one[0]) + product_right(minus_one_grad, w_one[1]),
        product_right(minus_one_grad, w_one[0]) - product_right(plus_one_grad, w_one[1]),
        product_right(plus_two_grad, w_two[0]) + product_right(minus_two_grad, w_two[1]),
        product_right(minus_two_grad, w_two[0]) - product_right(plus_two_grad, w_two[1])], axis=1).reshape(rows, -1, width)
    rotated_grad = (backward_parts * radial_rows.astype(jnp.float32)[:, None, :]).astype(jnp.bfloat16)
    source_grad = jnp.einsum("kje,ekc->ejc", rotation.astype(jnp.float32), rotated_grad.astype(jnp.float32)).astype(jnp.bfloat16)
    return source_grad, (grad_zero, grad_one, grad_two, grad_gate)


def reference(nodes, sources, targets, edge_counts, wigner, radial, cotangent, w_zero, w_one, w_two, w_gate):
    width = w_gate.shape[0]
    positions = jnp.arange(EDGES, dtype=jnp.int32)

    def one_batch(totals, items):
        node_rows, source_ids, target_ids, counts, rotation, radial_rows, upstream_rows = items
        valid = (positions % EDGE_DEV) < counts[positions // EDGE_DEV]
        gathered = jnp.take(node_rows, source_ids, axis=0).reshape(EDGES, -1, width)
        back, saved = edge_forward(gathered, rotation, radial_rows, valid, w_zero, w_one, w_two, w_gate)
        summed = jax.ops.segment_sum(back.reshape(EDGES, -1).astype(jnp.float32), target_ids, num_segments=NODES)
        upstream = jnp.take(upstream_rows, target_ids, axis=0) * valid[:, None].astype(upstream_rows.dtype)
        upstream = upstream.reshape(EDGES, -1, width)
        source_grad, grads = edge_backward(upstream, rotation, radial_rows, saved, w_zero, w_one, w_two, w_gate)
        grad_rows = jax.ops.segment_sum(source_grad.reshape(EDGES, -1).astype(jnp.float32), source_ids, num_segments=NODES)
        totals = tuple(total + grad for total, grad in zip(totals, grads))
        return totals, (summed.astype(jnp.bfloat16), grad_rows.astype(jnp.bfloat16))

    start_totals = (jnp.zeros(w_zero.shape, jnp.float32), jnp.zeros(w_one.shape, jnp.float32),
                    jnp.zeros(w_two.shape, jnp.float32), jnp.zeros(w_gate.shape, jnp.float32))
    totals, outputs = lax.scan(one_batch, start_totals,
                               (nodes, sources, targets, edge_counts, wigner, radial, cotangent))
    return outputs[0], outputs[1], totals[0], totals[1], totals[2], totals[3]
```

```python
import functools
import math

import jax
import jax.numpy as jnp
from jax import lax
from jax.experimental import pallas as pl
from jax.experimental.pallas import tpu as pltpu
from jax.sharding import PartitionSpec as P

F32 = jnp.float32
BF16 = jnp.bfloat16
VMEM_LIMIT = 48 * 1024 * 1024


def dot_nn(left, right):
    return jnp.dot(left, right, preferred_element_type=F32)


def dot_nt(left, right):
    return lax.dot_general(left, right, (((1,), (1,)), ((), ())), preferred_element_type=F32)


def dot_tn(left, right):
    return lax.dot_general(left, right, (((0,), (0,)), ((), ())), preferred_element_type=F32)


def kept_rows(degree, sizes):
    zero, one, two = sizes
    rows = [degree]
    if degree >= 1:
        rows += [zero + degree - 1, zero + one + degree - 1]
    if degree >= 2:
        rows += [zero + 2 * one + degree - 2, zero + 2 * one + two + degree - 2]
    return rows


def group_of(row, sizes):
    zero, one, two = sizes
    if row < zero:
        return 0, row
    if row < zero + 2 * one:
        return 1, row - zero
    return 2, row - zero - 2 * one


def widen(wigner_ref, wide_ref):
    for j in range(wigner_ref.shape[0]):
        wide_ref[j] = wigner_ref[j].astype(F32)


def fill_spread(degree, sizes, hits, wide_ref, spread_ref):
    nodes, edges = hits.shape
    for j in range(2 * degree + 1):
        for place, k in enumerate(kept_rows(degree, sizes)):
            row = wide_ref[degree * degree + j, k : k + 1, :]
            row = jnp.broadcast_to(row, (16, edges)).astype(BF16)
            for part in range(nodes // 16):
                at = j * nodes + part * 16
                spread_ref[at : at + 16, place * edges : (place + 1) * edges] = (
                    hits[part * 16 : (part + 1) * 16] * row
                )


def turn(pieces, sizes, hits, wide_ref, spreads, stacked, degree, width):
    nodes, edges = hits.shape
    orders = 2 * degree + 1
    spread_ref = spreads[degree % 2]
    fill_spread(degree, sizes, hits, wide_ref, spread_ref)
    for j in range(orders):
        column = (degree * degree + j) * width
        at = j * nodes
        for piece in pieces:
            stacked[at : at + piece.shape[0], :] = piece[:, column : column + width]
            at += piece.shape[0]
    count = len(kept_rows(degree, sizes))
    return dot_tn(stacked[0 : orders * nodes, :], spread_ref[0 : orders * nodes, 0 : count * edges])


def nodes_kernel(
    sizes, ids, sources, wigner, radial, first, gating, *refs
):
    pieces, (x_zero, x_one, x_two, scalar, gate), (wide, even, odd, stacked) = (
        refs[:-9],
        refs[-9:-4],
        refs[-4:],
    )
    width = gating.shape[0]
    edges = sources.shape[1]
    widen(wigner, wide)
    hits = (ids[...] == sources[...]).astype(F32).astype(BF16)
    scale = radial[...].astype(F32).T
    outs = (x_zero, x_one, x_two)
    for degree in range(sizes[0]):
        turned = turn(pieces, sizes, hits, wide, (even, odd), stacked, degree, width)
        for place, k in enumerate(kept_rows(degree, sizes)):
            group, row = group_of(k, sizes)
            outs[group][row * width : (row + 1) * width, :] = (
                turned[:, place * edges : (place + 1) * edges] * scale
            ).astype(BF16)
    low = dot_tn(first[...], x_zero[...])
    scalar[...] = low
    gate[...] = jax.nn.sigmoid(dot_tn(gating[...], low.astype(BF16)))


def cotangent_kernel(sizes, live, ids, targets, wigner, gate, *refs):
    pieces, (g_zero, g_one, g_two, head), (wide, even, odd, stacked) = (
        refs[:-8],
        refs[-8:-4],
        refs[-4:],
    )
    width, edges = gate.shape
    widen(wigner, wide)
    slots = lax.broadcasted_iota(jnp.int32, (1, edges), 1)
    wanted = jnp.where(slots < live[0], targets[...], -1)
    hits = (ids[...] == wanted).astype(F32).astype(BF16)
    outs = (g_zero, g_one, g_two)
    for degree in range(sizes[0]):
        turned = turn(pieces, sizes, hits, wide, (even, odd), stacked, degree, width)
        for place, k in enumerate(kept_rows(degree, sizes)):
            group, row = group_of(k, sizes)
            value = turned[:, place * edges : (place + 1) * edges]
            if k == 0:
                head[...] = value
                g_zero[0:width, :] = jnp.zeros((width, edges), BF16)
            else:
                outs[group][row * width : (row + 1) * width, :] = (value * gate[...]).astype(BF16)


def place_rows(shift, out, block, flat, values):
    rows = values.shape[0]
    step = math.gcd(math.gcd(block, flat), rows) if flat else math.gcd(block, rows)
    for at in range(0, rows, step):
        start = pl.multiple_of(flat + at + shift[(flat + at) // block], 16)
        out[pl.ds(start, step), :] = values[at : at + step]


def take_rows(shift, source, block, flat, rows, store):
    step = math.gcd(math.gcd(block, flat), rows) if flat else math.gcd(block, rows)
    for at in range(0, rows, step):
        start = pl.multiple_of(flat + at + shift[(flat + at) // block], 16)
        store(at, step, source[pl.ds(start, step), :])


def pair_grad_kernel(width, block, shift, x, g, out, total):
    half = x.shape[0] // 2
    flat = 0
    for part in range(2):
        if part == 0:
            total[...] = dot_nt(x[:half], g[:half]) + dot_nt(x[half:], g[half:])
        else:
            total[...] = dot_nt(x[:half], g[half:]) - dot_nt(x[half:], g[:half])
        for column in range(0, half, width):
            place_rows(shift, out, block, flat, total[:, column : column + width].astype(BF16))
            flat += half
    if flat < out.shape[0]:
        place_rows(shift, out, block, flat, jnp.zeros((out.shape[0] - flat, width), BF16))


def zero_grad_kernel(width, block, shift, x, g, out, total):
    rows = x.shape[0]
    total[...] = dot_nt(x[...], g[width:])
    flat = 0
    for column in range(0, rows - width, width):
        place_rows(shift, out, block, flat, total[:, column : column + width].astype(BF16))
        flat += rows
    if flat < out.shape[0]:
        place_rows(shift, out, block, flat, jnp.zeros((out.shape[0] - flat, width), BF16))


def message_kernel(
    sizes, live, targets, wigner, x_zero, x_one, x_two, g_zero, g_one, g_two, scalar, gate, head,
    w_zero, w_one, w_two, gating, partial, g_first, late, wide, even, odd, message, mixed
):
    width, edges = gate.shape
    zero, one, two = sizes
    nodes = partial.shape[0]
    widen(wigner, wide)

    def settle(group, first_row, count, total):
        inputs = (g_zero, g_one, g_two)[group]
        base = (0, zero, zero + 2 * one)[group]
        for row in range(count):
            k = base + first_row + row
            if k == 0:
                v = scalar[...]
                value = v * jax.nn.sigmoid(v)
            else:
                raw = mixed[row * width : (row + 1) * width, :]
                at = (first_row + row) * width
                total = total + raw * inputs[at : at + width, :].astype(F32)
                value = raw * gate[...]
            for degree in range(zero):
                rows = kept_rows(degree, sizes)
                if k in rows:
                    place = rows.index(k)
                    message[degree, :, place * edges : (place + 1) * edges] = value.astype(BF16)
        return total

    total = jnp.zeros((width, edges), F32)
    mixed[0 : zero * width, :] = dot_nn(w_zero[...], x_zero[...])
    total = settle(0, 0, zero, total)
    for group, size, x, w in ((1, one, x_one, w_one), (2, two, x_two, w_two)):
        half = size * width
        mixed[0:half, :] = dot_nn(w[0], x[:half]) - dot_nn(w[1], x[half:])
        total = settle(group, 0, size, total)
        mixed[0:half, :] = dot_nn(w[1], x[:half]) + dot_nn(w[0], x[half:])
        total = settle(group, size, size, total)

    gates = gate[...]
    gate_low = (total * (1.0 - gates)).astype(BF16)
    v = scalar[...]
    s = jax.nn.sigmoid(v)
    first = (head[...] * s * (1.0 + v * (1.0 - s)) + dot_nn(gating[...], gate_low)).astype(BF16)
    g_first[...] = first
    late[0 : zero * width, :] = dot_nt(x_zero[...], first)
    late[zero * width : (zero + 1) * width, :] = dot_nt(v.astype(BF16), gate_low)

    slots = lax.broadcasted_iota(jnp.int32, (1, edges), 1)
    wanted = jnp.where(slots < live[0], targets[...], -1)
    hits = lax.broadcasted_iota(jnp.int32, (nodes, edges), 0) == wanted
    scatter(sizes, hits, wide, (even, odd), message, partial, width)


def scatter(sizes, hits, wide, spreads, values, partial, width):
    hits = hits.astype(F32).astype(BF16)
    nodes, edges = hits.shape
    for degree in range(sizes[0]):
        spread_ref = spreads[degree % 2]
        fill_spread(degree, sizes, hits, wide, spread_ref)
        lanes = len(kept_rows(degree, sizes)) * edges
        orders = 2 * degree + 1
        summed = dot_nt(
            spread_ref[0 : orders * nodes, 0:lanes], values[degree, :, 0:lanes]
        ).astype(BF16)
        for j in range(orders):
            column = (degree * degree + j) * width
            partial[:, column : column + width] = summed[j * nodes : (j + 1) * nodes]


def source_kernel(
    sizes, sources, wigner, radial, g_first, g_zero, g_one, g_two, w_zero, w_one, w_two,
    partial, wide, even, odd, values, moved
):
    zero, one, two = sizes
    width, edges = g_first.shape
    nodes = partial.shape[0]
    widen(wigner, wide)
    scale = radial[...].astype(F32).T

    def settle(base, count):
        for row in range(count):
            k = base + row
            value = moved[row * width : (row + 1) * width, :] * scale
            for degree in range(zero):
                rows = kept_rows(degree, sizes)
                if k in rows:
                    place = rows.index(k)
                    values[degree, :, place * edges : (place + 1) * edges] = value.astype(BF16)

    moved[0 : zero * width, :] = dot_nn(w_zero[:, :width], g_first[...]) + dot_nn(
        w_zero[:, width:], g_zero[width:]
    )
    settle(0, zero)
    base = zero
    for size, g, w in ((one, g_one, w_one), (two, g_two, w_two)):
        half = size * width
        moved[0:half, :] = dot_nn(w[0], g[:half]) + dot_nn(w[1], g[half:])
        settle(base, size)
        moved[0:half, :] = dot_nn(w[0], g[half:]) - dot_nn(w[1], g[:half])
        settle(base + size, size)
        base += 2 * size
    hits = lax.broadcasted_iota(jnp.int32, (nodes, edges), 0) == sources[...]
    scatter(sizes, hits, wide, (even, odd), values, partial, width)


def pair_finish_kernel(width, block, shift, source, out):
    half = out.shape[1]
    flat = 0
    for part in range(2):
        for column in range(0, half, width):

            def store(at, step, rows, part=part, column=column):
                out[part, at : at + step, column : column + width] = rows.astype(F32)

            take_rows(shift, source, block, flat, half, store)
            flat += half


def zero_finish_kernel(width, block, shift, source, first, out):
    rows = out.shape[0]
    out[:, 0:width] = first[0:rows, :]
    flat = 0
    for column in range(width, rows, width):

        def store(at, step, values, column=column):
            out[at : at + step, column : column + width] = values.astype(F32)

        take_rows(shift, source, block, flat, rows, store)
        flat += rows


SMEM = pl.BlockSpec(memory_space=pltpu.SMEM)
VMEM = pl.BlockSpec(memory_space=pltpu.VMEM)


def call(kernel, out_shape, args, scratch=(), smem=0, flops=0, moved=0):
    return pl.pallas_call(
        kernel,
        out_shape=out_shape,
        in_specs=[SMEM] * smem + [VMEM] * (len(args) - smem),
        out_specs=jax.tree.map(lambda _: VMEM, out_shape),
        scratch_shapes=list(scratch),
        compiler_params=pltpu.CompilerParams(vmem_limit_bytes=VMEM_LIMIT),
        cost_estimate=pl.CostEstimate(
            flops=int(flops), bytes_accessed=int(moved), transcendentals=0
        ),
    )(*args)


def shaped(shape, dtype):
    return jax.ShapeDtypeStruct(shape, dtype)


def exchange(value, axis, bit):
    count = lax.axis_size(axis)
    return lax.ppermute(value, axis, [(i, i ^ bit) for i in range(count)])


def bits_of(axis):
    count = lax.axis_size(axis)
    return [(axis, 1 << b) for b in range(count.bit_length() - 1)]


def relative_gather(shard):
    order = [0]
    held = [shard]
    for axis, bit in bits_of("graph")[::-1]:
        block = held[0] if len(held) == 1 else jnp.concatenate(held, axis=0)
        held = [block, exchange(block, axis, bit)]
        order = order + [o ^ bit for o in order]
    return held, order


def block_shift(stages, blocks, block):
    mine = jnp.int32(0)
    for axis, bit in stages:
        mine = 2 * mine + ((lax.axis_index(axis) & bit) != 0).astype(jnp.int32)
    at = jnp.arange(blocks, dtype=jnp.int32)
    return ((at ^ mine) - at) * block


def sum_rows(value, stages):
    for axis, bit in stages:
        half = value.shape[0] // 2
        other = exchange(value[half:], axis, bit)
        value = (value[:half].astype(F32) + other.astype(F32)).astype(BF16)
    for axis, bit in stages[::-1]:
        value = jnp.concatenate([value, exchange(value, axis, bit)], axis=0)
    return value


def per_device(
    nodes, sources, targets, edge_counts, wigner, radial, cotangent, w_zero, w_one, w_two, w_gate
):
    width = w_gate.shape[0]
    zero, one, two = w_zero.shape[0] // width, w_one.shape[1] // width, w_two.shape[1] // width
    sizes = (zero, one, two)
    shard = nodes.shape[1]
    node_count = shard * lax.axis_size("graph")
    edges = sources.shape[1]
    coefficients = wigner.shape[2]
    kept = wigner.shape[1]
    features = nodes.shape[2]
    live = edge_counts[0]
    rotation = jnp.transpose(wigner[0], (1, 0, 2))
    radial_rows = radial[0]

    node_blocks, order = relative_gather(nodes[0])
    upstream_blocks, _ = relative_gather(cotangent[0])
    ids = (jnp.array(order, jnp.int32) ^ lax.axis_index("graph"))[:, None] * shard
    ids = (ids + jnp.arange(shard, dtype=jnp.int32)[None, :]).reshape(node_count, 1)

    pairs = 2 * zero - 1
    spread = [
        pltpu.VMEM(((2 * d + 1) * node_count, 5 * edges), BF16) for d in (zero - 1, zero - 2)
    ]
    if zero % 2 == 0:
        spread = spread[::-1]
    wide = pltpu.VMEM((coefficients, kept, edges), F32)
    turning = [wide, *spread, pltpu.VMEM((pairs * node_count, width), BF16)]
    turn_cost = 2 * coefficients * 5 * node_count * width * edges
    edge_flops = 2 * edges * width * width * (zero * zero + 4 * one * one + 4 * two * two)
    rows = [zero * width, 2 * one * width, 2 * two * width]
    wide_rows = [shaped((r, edges), BF16) for r in rows]
    one_row = shaped((width, edges), F32)
    wigner_bytes = rotation.size * 2

    x_zero, x_one, x_two, scalar, gate = call(
        functools.partial(nodes_kernel, sizes),
        (*wide_rows, one_row, one_row),
        [ids, sources, rotation, radial_rows, w_zero[:, :width], w_gate, *node_blocks],
        turning,
        flops=turn_cost,
        moved=wigner_bytes + 2 * sum(rows) * edges,
    )
    g_zero, g_one, g_two, head = call(
        functools.partial(cotangent_kernel, sizes),
        (*wide_rows, one_row),
        [live, ids, targets, rotation, gate, *upstream_blocks],
        turning,
        smem=1,
        flops=turn_cost,
        moved=wigner_bytes + 2 * sum(rows) * edges,
    )

    dp_bits = bits_of("dp")
    forward = dp_bits + bits_of("graph")
    other_way = dp_bits[:1] + dp_bits[1:][::-1] + bits_of("graph")
    blocks = lax.axis_size("dp") * lax.axis_size("graph")

    def padded(count):
        return -(-count // (16 * blocks)) * 16

    def summed_pair(x, g, stages, size):
        side = size * width
        block = padded(2 * size * side)
        shift = block_shift(stages, blocks, block)
        partial = call(
            functools.partial(pair_grad_kernel, width, block),
            shaped((blocks * block, width), BF16),
            [shift, x, g],
            [pltpu.VMEM((side, side), F32)],
            smem=1,
            flops=8 * side * side * edges,
            moved=8 * side * side,
        )
        total = sum_rows(partial, stages)
        return call(
            functools.partial(pair_finish_kernel, width, block),
            shaped((2, side, side), F32),
            [shift, total],
            smem=1,
            moved=12 * side * side,
        )

    grad_two = summed_pair(x_two, g_two, forward, two)
    grad_one = summed_pair(x_one, g_one, other_way, one)

    side = zero * width
    zero_block = padded(side * (zero - 1))
    zero_shift = block_shift(forward, blocks, zero_block)
    zero_partial = call(
        functools.partial(zero_grad_kernel, width, zero_block),
        shaped((blocks * zero_block, width), BF16),
        [zero_shift, x_zero, g_zero],
        [pltpu.VMEM((side, side - width), F32)],
        smem=1,
        flops=2 * side * side * edges,
        moved=4 * side * side,
    )
    zero_total = sum_rows(zero_partial, forward)

    messages = pltpu.VMEM((zero, width, 5 * edges), BF16)
    products = pltpu.VMEM((zero * width, edges), F32)
    partial_shape = shaped((node_count, features), BF16)
    partial, g_first, late = call(
        functools.partial(message_kernel, sizes),
        (partial_shape, shaped((width, edges), BF16), shaped((side + width, width), F32)),
        [
            live, targets, rotation, x_zero, x_one, x_two, g_zero, g_one, g_two, scalar, gate, head,
            w_zero.T, jnp.swapaxes(w_one, 1, 2), jnp.swapaxes(w_two, 1, 2), w_gate,
        ],
        [wide, *spread, messages, products],
        smem=1,
        flops=edge_flops + turn_cost,
        moved=wigner_bytes + 4 * sum(rows) * edges,
    )
    summed = lax.psum_scatter(partial, "graph", scatter_dimension=0, tiled=True)
    late = lax.psum(late, ("dp", "graph"))
    grad_partial = call(
        functools.partial(source_kernel, sizes),
        partial_shape,
        [sources, rotation, radial_rows, g_first, g_zero, g_one, g_two, w_zero, w_one, w_two],
        [wide, *spread, messages, products],
        flops=edge_flops + turn_cost,
        moved=wigner_bytes + 2 * sum(rows) * edges,
    )
    grad_rows = lax.psum_scatter(grad_partial, "graph", scatter_dimension=0, tiled=True)
    grad_zero = call(
        functools.partial(zero_finish_kernel, width, zero_block),
        shaped((side, side), F32),
        [zero_shift, zero_total, late],
        smem=1,
        moved=6 * side * side,
    )
    return (summed[None], grad_rows[None], grad_zero, grad_one, grad_two, late[side:])


def solution(mesh):
    in_specs = (
        P("dp", "graph", None),
        P("dp", "graph"),
        P("dp", "graph"),
        P("dp", "graph"),
        P("dp", None, None, "graph"),
        P("dp", "graph", None),
        P("dp", "graph", None),
        P(),
        P(),
        P(),
        P(),
    )
    out_specs = (P("dp", "graph", None), P("dp", "graph", None), P(), P(), P(), P())
    return jax.shard_map(
        per_device, mesh=mesh, in_specs=in_specs, out_specs=out_specs, check_vma=False
    )
```

```python
import functools
import math

import jax
import jax.numpy as jnp
from jax import lax
from jax.experimental import pallas as pl
from jax.experimental.pallas import tpu as pltpu
from jax.sharding import PartitionSpec as P

F32 = jnp.float32
BF16 = jnp.bfloat16
SPARE_VMEM = 8 * 1024 * 1024


def dot_nn(left, right):
    return jnp.dot(left, right, preferred_element_type=F32)


def dot_nt(left, right):
    return lax.dot_general(left, right, (((1,), (1,)), ((), ())), preferred_element_type=F32)


def dot_tn(left, right):
    return lax.dot_general(left, right, (((0,), (0,)), ((), ())), preferred_element_type=F32)


def kept_rows(degree, sizes):
    zero, one, two = sizes
    rows = [degree]
    if degree >= 1:
        rows += [zero + degree - 1, zero + one + degree - 1]
    if degree >= 2:
        rows += [zero + 2 * one + degree - 2, zero + 2 * one + two + degree - 2]
    return rows


def group_of(row, sizes):
    zero, one, two = sizes
    if row < zero:
        return 0, row
    if row < zero + 2 * one:
        return 1, row - zero
    return 2, row - zero - 2 * one


class Copies:
    def __init__(self, semaphores):
        self.semaphores = semaphores
        self.count = 0

    def start(self, sources, targets):
        started = []
        for source, target in zip(sources, targets):
            copy = pltpu.make_async_copy(source, target, self.semaphores.at[self.count])
            copy.start()
            self.count += 1
            started.append(copy)
        return started


def wait(started):
    for copy in started:
        copy.wait()


def prepare_kernel(
    wigner_hbm, w_zero_hbm, w_one_hbm, w_two_hbm, radial, wide, scale, t_zero, t_one, t_two,
    wigner, w_zero, w_one, w_two, semaphores
):
    copies = Copies(semaphores)
    first = copies.start((wigner_hbm, w_zero_hbm), (wigner, w_zero))
    rest = copies.start((w_one_hbm, w_two_hbm), (w_one, w_two))
    scale[...] = radial[...].astype(F32).T
    wait(first)
    for j in range(wigner.shape[0]):
        wide[j] = wigner[j].astype(F32)
    t_zero[...] = w_zero[...].T
    wait(rest)
    for part in range(2):
        t_one[part] = w_one[part].T
        t_two[part] = w_two[part].T


def fill_spread(degree, sizes, hits, wide_ref, spread_ref):
    nodes, edges = hits.shape
    for j in range(2 * degree + 1):
        for place, k in enumerate(kept_rows(degree, sizes)):
            row = wide_ref[degree * degree + j, k : k + 1, :]
            row = jnp.broadcast_to(row, (16, edges)).astype(BF16)
            for part in range(nodes // 16):
                at = j * nodes + part * 16
                spread_ref[at : at + 16, place * edges : (place + 1) * edges] = (
                    hits[part * 16 : (part + 1) * 16] * row
                )


def turn(pieces, sizes, hits, wide_ref, spreads, stacked, degree, width):
    nodes, edges = hits.shape
    orders = 2 * degree + 1
    spread_ref = spreads[degree % 2]
    fill_spread(degree, sizes, hits, wide_ref, spread_ref)
    for j in range(orders):
        column = (degree * degree + j) * width
        at = j * nodes
        for piece in pieces:
            stacked[at : at + piece.shape[0], :] = piece[:, column : column + width]
            at += piece.shape[0]
    count = len(kept_rows(degree, sizes))
    return dot_tn(stacked[0 : orders * nodes, :], spread_ref[0 : orders * nodes, 0 : count * edges])


def nodes_kernel(sizes, order, sources, wide, scale, first, gating, *refs):
    pieces, (x_zero, x_one, x_two, scalar, gate), (even, odd, stacked) = (
        refs[:-8],
        refs[-8:-3],
        refs[-3:],
    )
    width = gating.shape[0]
    edges = sources.shape[1]
    hits = shard_hits(order, pieces[0].shape[0], sources[...])
    outs = (x_zero, x_one, x_two)
    for degree in range(sizes[0]):
        turned = turn(pieces, sizes, hits, wide, (even, odd), stacked, degree, width)
        for place, k in enumerate(kept_rows(degree, sizes)):
            group, row = group_of(k, sizes)
            outs[group][row * width : (row + 1) * width, :] = (
                turned[:, place * edges : (place + 1) * edges] * scale[...]
            ).astype(BF16)
    low = dot_nn(first[...], x_zero[...])
    scalar[...] = low
    gate[...] = jax.nn.sigmoid(dot_tn(gating[...], low.astype(BF16)))


def products_kernel(
    sizes, x_zero, x_one, x_two, scalar, gate, w_zero, w_one, w_two,
    m_zero, m_one, m_two, messages, mixed
):
    width, edges = gate.shape
    zero, one, two = sizes

    def settle(out, first_row, base, count):
        for row in range(count):
            k = base + row
            at = (first_row + row) * width
            raw = mixed[row * width : (row + 1) * width, :]
            out[at : at + width, :] = raw.astype(BF16)
            if k == 0:
                v = scalar[...]
                value = v * jax.nn.sigmoid(v)
            else:
                value = raw * gate[...]
            store_row(messages, sizes, k, value)

    mixed[0 : zero * width, :] = dot_nn(w_zero[...], x_zero[...])
    settle(m_zero, 0, 0, zero)
    base = zero
    for size, x, w, out in ((one, x_one, w_one, m_one), (two, x_two, w_two, m_two)):
        half = size * width
        mixed[0:half, :] = dot_nn(w[0], x[:half]) - dot_nn(w[1], x[half:])
        settle(out, 0, base, size)
        mixed[0:half, :] = dot_nn(w[1], x[:half]) + dot_nn(w[0], x[half:])
        settle(out, size, base + size, size)
        base += 2 * size


def store_row(values, sizes, k, value):
    edges = value.shape[1]
    for degree in range(sizes[0]):
        rows = kept_rows(degree, sizes)
        if k in rows:
            place = rows.index(k)
            values[degree, :, place * edges : (place + 1) * edges] = value.astype(BF16)


def shard_hits(order, shard, index):
    mine = lax.axis_index("graph")
    rows = lax.broadcasted_iota(jnp.int32, (shard, index.shape[1]), 0)
    hits = [(rows + (other ^ mine) * shard == index).astype(F32).astype(BF16) for other in order]
    return jnp.concatenate(hits, axis=0)


def only_live(live, index):
    slots = lax.broadcasted_iota(jnp.int32, index.shape, 1)
    return jnp.where(slots < live[0], index[...], -1)


def place_of(stages):
    mine = jnp.int32(0)
    for axis, bit in stages:
        mine = 2 * mine + jnp.where((lax.axis_index(axis) & bit) != 0, 1, 0)
    return mine


def cotangent_kernel(
    sizes, order, live, targets, wide, scalar, gate, gating, m_zero, m_one, m_two, *refs
):
    pieces, (g_zero, g_one, g_two, gate_low), (even, odd, stacked, total, head) = (
        refs[:-9],
        refs[-9:-5],
        refs[-5:],
    )
    width, edges = gate.shape
    hits = shard_hits(order, pieces[0].shape[0], only_live(live, targets))
    outs = (g_zero, g_one, g_two)
    mixed = (m_zero, m_one, m_two)
    total[...] = jnp.zeros((width, edges), F32)
    for degree in range(sizes[0]):
        turned = turn(pieces, sizes, hits, wide, (even, odd), stacked, degree, width)
        for place, k in enumerate(kept_rows(degree, sizes)):
            group, row = group_of(k, sizes)
            value = turned[:, place * edges : (place + 1) * edges]
            if k == 0:
                head[...] = value
            else:
                at = row * width
                value = value * gate[...]
                outs[group][at : at + width, :] = value.astype(BF16)
                total[...] += value * mixed[group][at : at + width, :].astype(F32)
    low = (total[...] * (1.0 - gate[...])).astype(BF16)
    gate_low[...] = low
    v = scalar[...]
    s = jax.nn.sigmoid(v)
    first = head[...] * s * (1.0 + v * (1.0 - s)) + dot_nn(gating[...], low)
    g_zero[0:width, :] = first.astype(BF16)


def runs(block, flat, rows):
    at = 0
    while at < rows:
        step = min(rows - at, block - (flat + at) % block)
        yield at, step, (flat + at) // block
        at += step


def place_rows(mine, out, block, flat, values):
    for at, step, index in runs(block, flat, values.shape[0]):
        start = pl.multiple_of(flat + at + ((index ^ mine) - index) * block, 16)
        out[pl.ds(start, step), :] = values[at : at + step]


def place_matrix(mine, out, block, flat, total, rows, columns, width):
    for column in range(0, columns, width):
        place_rows(mine, out, block, flat, total[0:rows, column : column + width].astype(BF16))
        flat += rows
    return flat


def finish_rows(mine, out, block, flat, kept, sent):
    rows, width = out.shape
    if flat < rows:
        place_rows(mine, out, block, flat, jnp.zeros((rows - flat, width), BF16))
    kept[...] = out[: rows // 2]
    sent[...] = out[rows // 2 :]


def grad_a_kernel(block, stages, x_two, g_two, x_one, g_one, kept, sent, out, total):
    mine = place_of(stages)
    width = out.shape[1]
    half = x_two.shape[0] // 2
    total[0:half, 0:half] = dot_nt(x_two[:half], g_two[:half]) + dot_nt(x_two[half:], g_two[half:])
    flat = place_matrix(mine, out, block, 0, total, half, half, width)
    total[0:half, 0:half] = dot_nt(x_two[:half], g_two[half:]) - dot_nt(x_two[half:], g_two[:half])
    flat = place_matrix(mine, out, block, flat, total, half, half, width)
    half = x_one.shape[0] // 2
    total[0:half, 0:half] = dot_nt(x_one[:half], g_one[:half]) + dot_nt(x_one[half:], g_one[half:])
    flat = place_matrix(mine, out, block, flat, total, half, half, width)
    finish_rows(mine, out, block, flat, kept, sent)


def grad_b_kernel(
    block, stages, x_one, g_one, x_zero, g_zero, scalar, gate_low, kept, sent, out, total
):
    mine = place_of(stages)
    width = out.shape[1]
    half = x_one.shape[0] // 2
    total[0:half, 0:half] = dot_nt(x_one[:half], g_one[half:]) - dot_nt(x_one[half:], g_one[:half])
    flat = place_matrix(mine, out, block, 0, total, half, half, width)
    rows = x_zero.shape[0]
    total[...] = dot_nt(x_zero[...], g_zero[...])
    flat = place_matrix(mine, out, block, flat, total, rows, rows, width)
    gate_grad = dot_nt(scalar[...].astype(BF16), gate_low[...]).astype(BF16)
    place_rows(mine, out, block, flat, gate_grad)
    finish_rows(mine, out, block, flat + width, kept, sent)


def spread_back(sizes, hits, wide, spreads, values, kept, sent):
    width = values.shape[1]
    half = kept.shape[0]
    nodes, edges = hits.shape
    for degree in range(sizes[0]):
        spread_ref = spreads[degree % 2]
        fill_spread(degree, sizes, hits, wide, spread_ref)
        lanes = len(kept_rows(degree, sizes)) * edges
        orders = 2 * degree + 1
        summed = dot_nt(
            spread_ref[0 : orders * nodes, 0:lanes], values[degree, :, 0:lanes]
        ).astype(BF16)
        for j in range(orders):
            column = (degree * degree + j) * width
            kept[:, column : column + width] = summed[j * nodes : j * nodes + half]
            sent[:, column : column + width] = summed[j * nodes + half : (j + 1) * nodes]


def back_kernel(
    sizes, order, live, w_zero_hbm, w_one_hbm, w_two_hbm, sources, targets, wide, scale, messages,
    g_zero, g_one, g_two, sum_kept, sum_sent, grad_kept, grad_sent,
    w_zero, w_one, w_two, even, odd, values, moved, semaphores
):
    copies = Copies(semaphores)
    given = copies.start((w_zero_hbm, w_one_hbm, w_two_hbm), (w_zero, w_one, w_two))
    shard = 2 * sum_kept.shape[0] // len(order)
    hits = shard_hits(order, shard, only_live(live, targets))
    spread_back(sizes, hits, wide, (even, odd), messages, sum_kept, sum_sent)

    zero, one, two = sizes
    width = scale.shape[0]

    def settle(base, count):
        for row in range(count):
            value = moved[row * width : (row + 1) * width, :] * scale[...]
            store_row(values, sizes, base + row, value)

    wait(given)
    moved[0 : zero * width, :] = dot_nn(w_zero[...], g_zero[...])
    settle(0, zero)
    base = zero
    for size, g, w in ((one, g_one, w_one), (two, g_two, w_two)):
        half = size * width
        moved[0:half, :] = dot_nn(w[0], g[:half]) + dot_nn(w[1], g[half:])
        settle(base, size)
        moved[0:half, :] = dot_nn(w[0], g[half:]) - dot_nn(w[1], g[:half])
        settle(base + size, size)
        base += 2 * size
    hits = shard_hits(order, shard, sources[...])
    spread_back(sizes, hits, wide, (even, odd), values, grad_kept, grad_sent)


def take_matrix(mine, joined, block, flat, rows, columns, out):
    width = joined.shape[1]
    for column in range(0, columns, width):
        for at, step, index in runs(block, flat, rows):
            start = pl.multiple_of(flat + at + ((index ^ mine) - index) * block, 16)
            out[at : at + step, column : column + width] = joined[pl.ds(start, step), :].astype(F32)
        flat += rows
    return flat


def join(low, high, joined):
    rows = low.shape[0]
    joined[0:rows, :] = low[...]
    joined[rows:, :] = high[...]


def finish_two_kernel(block, stages, low, high, result, out, joined, semaphores):
    half = out.shape[1]
    copies = Copies(semaphores)
    join(low, high, joined)
    flat, started = 0, []
    for part in range(2):
        flat = take_matrix(place_of(stages), joined, block, flat, half, half, out.at[part])
        started += copies.start((out.at[part],), (result.at[part],))
    wait(started)


def finish_kernel(
    block, skip_a, skip_b, stages_a, stages_b, low_a, high_a, low_b, high_b,
    one_result, zero_result, gate_result, one, zero, gate, joined, semaphores
):
    half = one.shape[1]
    copies = Copies(semaphores)
    join(low_a, high_a, joined)
    take_matrix(place_of(stages_a), joined, block, skip_a, half, half, one.at[0])
    started = copies.start((one.at[0],), (one_result.at[0],))
    join(low_b, high_b, joined)
    mine = place_of(stages_b)
    take_matrix(mine, joined, block, 0, half, half, one.at[1])
    started += copies.start((one.at[1],), (one_result.at[1],))
    side = zero.shape[0]
    flat = take_matrix(mine, joined, block, skip_b, side, side, zero)
    started += copies.start((zero,), (zero_result,))
    take_matrix(mine, joined, block, flat, gate.shape[0], gate.shape[1], gate)
    started += copies.start((gate,), (gate_result,))
    wait(started)


SMEM = pl.BlockSpec(memory_space=pltpu.SMEM)
VMEM = pl.BlockSpec(memory_space=pltpu.VMEM)
ANY = pl.BlockSpec(memory_space=pl.ANY)


def call(kernel, out_shape, args, scratch=(), smem=0, hbm=0, copies=0, flops=0, moved=0):
    vmem = [pltpu.with_memory_space_constraint(a, pltpu.VMEM) for a in args[smem + hbm :]]
    held = sum(math.prod(a.shape) * jnp.dtype(a.dtype).itemsize for a in scratch)
    held += held // 8
    if copies:
        scratch = [*scratch, pltpu.SemaphoreType.DMA((copies,))]
    return pl.pallas_call(
        kernel,
        out_shape=out_shape,
        in_specs=[SMEM] * smem + [ANY] * hbm + [VMEM] * len(vmem),
        out_specs=tuple(ANY if isinstance(o, jax.ShapeDtypeStruct) else VMEM for o in out_shape),
        scratch_shapes=list(scratch),
        compiler_params=pltpu.CompilerParams(vmem_limit_bytes=held + SPARE_VMEM),
        cost_estimate=pl.CostEstimate(
            flops=int(flops), bytes_accessed=int(moved), transcendentals=0
        ),
    )(*args[: smem + hbm], *vmem)


def shaped(shape, dtype):
    return jax.ShapeDtypeStruct(shape, dtype)


def exchange(value, axis, bit):
    count = lax.axis_size(axis)
    return lax.ppermute(value, axis, [(i, i ^ bit) for i in range(count)])


def bits_of(axis):
    count = lax.axis_size(axis)
    return [(axis, 1 << b) for b in range(count.bit_length() - 1)]


def relative_gather(shards, beside):
    order, held = [0], [[shard] for shard in shards]
    for axis, bit in bits_of("graph")[::-1]:
        held = [blocks + [exchange(block, axis, bit) for block in blocks] for blocks in held]
        order = order + [o ^ bit for o in order]
        if len(order) == 2:
            held[0][1], *beside = tied(held[0][1], *beside)
    return held, order, beside


def relative_sum(arrays, stages):
    for axis, bit in stages:
        half = arrays[0].shape[0] // 2
        sent = jnp.concatenate([rows[half:] for rows in arrays], axis=0)
        other = exchange(sent, axis, bit)
        arrays = [
            add_low(rows[:half], other[at * half : (at + 1) * half])
            for at, rows in enumerate(arrays)
        ]
    return arrays


def tied(*values):
    return lax.optimization_barrier(values)


def add_low(kept, other):
    return (kept.astype(F32) + other.astype(F32)).astype(BF16)


def per_device(
    nodes, sources, targets, edge_counts, wigner, radial, cotangent, w_zero, w_one, w_two, w_gate
):
    width = w_gate.shape[0]
    zero, one, two = w_zero.shape[0] // width, w_one.shape[1] // width, w_two.shape[1] // width
    sizes = (zero, one, two)
    shard = nodes.shape[1]
    node_count = shard * lax.axis_size("graph")
    edges = sources.shape[1]
    coefficients = wigner.shape[2]
    kept = wigner.shape[1]
    features = nodes.shape[2]
    live = edge_counts[0]
    rotation = jnp.transpose(wigner[0], (1, 0, 2))
    radial_rows = radial[0]

    pairs = 2 * zero - 1
    spread = [
        pltpu.VMEM(((2 * d + 1) * node_count, 5 * edges), BF16) for d in (zero - 1, zero - 2)
    ]
    if zero % 2 == 0:
        spread = spread[::-1]
    stacked = pltpu.VMEM((pairs * node_count, width), BF16)
    edge_block = pltpu.VMEM((width, edges), F32)
    turn_cost = 2 * coefficients * 5 * node_count * width * edges
    edge_flops = 2 * edges * width * width * (zero * zero + 4 * one * one + 4 * two * two)
    rows = [zero * width, 2 * one * width, 2 * two * width]
    wide_rows = [pltpu.VMEM((r, edges), BF16) for r in rows]
    values_shape = pltpu.VMEM((zero, width, 5 * edges), BF16)
    products = pltpu.VMEM((zero * width, edges), F32)
    partial_shape = pltpu.VMEM((node_count // 2, features), BF16)
    weights = [pltpu.VMEM(w.shape, BF16) for w in (w_zero, w_one, w_two)]

    prepared = call(
        prepare_kernel,
        (pltpu.VMEM(rotation.shape, F32), edge_block, *weights),
        [rotation, w_zero, w_one, w_two, radial_rows],
        [pltpu.VMEM(rotation.shape, BF16), *weights],
        hbm=4,
        copies=4,
        moved=rotation.size * 8 + edge_flops / edges,
    )
    (node_blocks, upstream_blocks), order, prepared = relative_gather(
        (nodes[0], cotangent[0]), prepared
    )
    wide, scale, *turned = prepared
    node_blocks[0], *upstream_blocks[:2] = tied(node_blocks[0], *upstream_blocks[:2])
    x_zero, x_one, x_two, scalar, gate = call(
        functools.partial(nodes_kernel, sizes, order),
        (*wide_rows, edge_block, edge_block),
        [sources, wide, scale, turned[0][:width], w_gate, *node_blocks],
        [*spread, stacked],
        flops=turn_cost,
        moved=4 * sum(rows) * edges,
    )
    m_zero, m_one, m_two, messages = call(
        functools.partial(products_kernel, sizes),
        (*wide_rows, values_shape),
        [x_zero, x_one, x_two, scalar, gate, *turned],
        [products],
        flops=edge_flops,
        moved=6 * sum(rows) * edges,
    )
    g_zero, g_one, g_two, gate_low = call(
        functools.partial(cotangent_kernel, sizes, order),
        (*wide_rows, pltpu.VMEM((width, edges), BF16)),
        [live, targets, wide, scalar, gate, w_gate, m_zero, m_one, m_two]
        + upstream_blocks,
        [*spread, stacked, edge_block, edge_block],
        smem=1,
        flops=turn_cost,
        moved=4 * sum(rows) * edges,
    )

    dp_bits = bits_of("dp")
    stages_a = dp_bits + bits_of("graph")
    stages_b = dp_bits[:1] + dp_bits[1:][::-1] + bits_of("graph")
    blocks = lax.axis_size("dp") * lax.axis_size("graph")
    rows_two = 2 * two * two * width
    rows_one = one * one * width
    rows_zero = zero * zero * width
    most = max(rows_two + rows_one, rows_one + rows_zero + width)
    block = -(-most // (16 * blocks)) * 16
    half_list = pltpu.VMEM((blocks * block // 2, width), BF16)
    whole_list = pltpu.VMEM((blocks * block, width), BF16)
    side = zero * width
    square = pltpu.VMEM((side, side), F32)
    a, sent_a = call(
        functools.partial(grad_a_kernel, block, stages_a),
        (half_list, half_list),
        [x_two, g_two, x_one, g_one],
        [whole_list, square],
        flops=edge_flops / 2,
        moved=4 * blocks * block * width,
    )
    b, sent_b = call(
        functools.partial(grad_b_kernel, block, stages_b),
        (half_list, half_list),
        [x_one, g_one, x_zero, g_zero, scalar, gate_low],
        [whole_list, square],
        flops=edge_flops / 2,
        moved=4 * blocks * block * width,
    )

    graph_bits = bits_of("graph")
    last = len(dp_bits) - 1
    for place, (stage_a, stage_b) in enumerate(zip(stages_a, stages_b)):
        if place > 0:
            half = a.shape[0] // 2
            a, sent_a, b, sent_b = a[:half], a[half:], b[:half], b[half:]
        if place <= last:
            other_a, other_b = exchange(sent_a, *stage_a), exchange(sent_b, *stage_b)
        else:
            other = exchange(jnp.concatenate([sent_a, sent_b], axis=0), *stage_a)
            other_a, other_b = other[:half], other[half:]
        if place == 0:
            a, b = add_low(a, other_a), add_low(b, other_b)
            a, b, messages = tied(a, b, messages)
            sum_kept, sum_sent, grad_kept, grad_sent = call(
                functools.partial(back_kernel, sizes, order),
                (partial_shape,) * 4,
                [
                    live, w_zero, w_one, w_two, sources, targets, wide, scale, messages,
                    g_zero, g_one, g_two,
                ],
                [*weights, *spread, pltpu.VMEM(values_shape.shape, BF16), products],
                smem=1,
                hbm=3,
                copies=3,
                flops=edge_flops + 2 * turn_cost,
                moved=8 * sum(rows) * edges,
            )
            continue
        if place == 1:
            other_a, other_b, sum_kept, sum_sent, grad_kept, grad_sent = tied(
                other_a, other_b, sum_kept, sum_sent, grad_kept, grad_sent
            )
            sum_half = add_low(sum_kept, exchange(sum_sent, *graph_bits[0]))
        if place == last:
            other_a, other_b, sum_half = tied(other_a, other_b, sum_half)
        a, b = add_low(a, other_a), add_low(b, other_b)
    ab = jnp.concatenate([a, b], axis=0)
    for stage in stages_a[:last:-1]:
        half = ab.shape[0] // 2
        other = exchange(ab, *stage)
        ab = jnp.concatenate([ab[:half], other[:half], ab[half:], other[half:]], axis=0)
    ab, grad_kept, grad_sent, sum_half = tied(ab, grad_kept, grad_sent, sum_half)
    grad_half = add_low(grad_kept, exchange(grad_sent, *graph_bits[0]))
    half = ab.shape[0] // 2
    a, b = ab[:half], ab[half:]
    for place in range(len(dp_bits))[::-1]:
        half_a = (a, exchange(a, *stages_a[place]))
        half_b = (b, exchange(b, *stages_b[place]))
        if place == last:
            (low_a, high_a), (low_b, high_b) = half_a, half_b
            high_a, high_b, grad_half = tied(high_a, high_b, grad_half)
            half_a, half_b = (low_a, high_a), (low_b, high_b)
            both = relative_sum([sum_half, grad_half], graph_bits[1:])
        if place > 0:
            a, b = jnp.concatenate(half_a, axis=0), jnp.concatenate(half_b, axis=0)
    summed, grad_rows = both

    two_shape = (2, two * width, two * width)
    one_shape = (2, one * width, one * width)
    (grad_two,) = call(
        functools.partial(finish_two_kernel, block, stages_a),
        (shaped(two_shape, F32),),
        [*half_a],
        [pltpu.VMEM(two_shape, F32), whole_list],
        copies=2,
        moved=6 * rows_two * width,
    )
    grad_one, grad_zero, grad_gate = call(
        functools.partial(finish_kernel, block, rows_two, rows_one, stages_a, stages_b),
        (shaped(one_shape, F32), shaped((side, side), F32), shaped((width, width), F32)),
        [*half_a, *half_b],
        [pltpu.VMEM(one_shape, F32), square, pltpu.VMEM((width, width), F32), whole_list],
        copies=4,
        moved=12 * rows_one * width,
    )
    return (summed[None], grad_rows[None], grad_zero, grad_one, grad_two, grad_gate)


def solution(mesh):
    in_specs = (
        P("dp", "graph", None),
        P("dp", "graph"),
        P("dp", "graph"),
        P("dp", "graph"),
        P("dp", None, None, "graph"),
        P("dp", "graph", None),
        P("dp", "graph", None),
        P(),
        P(),
        P(),
        P(),
    )
    out_specs = (P("dp", "graph", None), P("dp", "graph", None), P(), P(), P(), P())
    return jax.shard_map(
        per_device, mesh=mesh, in_specs=in_specs, out_specs=out_specs, check_vma=False
    )
```

```python
import functools
import math

import jax
import jax.numpy as jnp
from jax import lax
from jax.experimental import pallas as pl
from jax.experimental.pallas import tpu as pltpu
from jax.sharding import PartitionSpec as P

F32 = jnp.float32
BF16 = jnp.bfloat16
SPARE_VMEM = 8 * 1024 * 1024


def dot_nn(left, right):
    return jnp.dot(left, right, preferred_element_type=F32)


def dot_nt(left, right):
    return lax.dot_general(left, right, (((1,), (1,)), ((), ())), preferred_element_type=F32)


def dot_tn(left, right):
    return lax.dot_general(left, right, (((0,), (0,)), ((), ())), preferred_element_type=F32)


def kept_rows(degree, sizes):
    zero, one, two = sizes
    rows = [degree]
    if degree >= 1:
        rows += [zero + degree - 1, zero + one + degree - 1]
    if degree >= 2:
        rows += [zero + 2 * one + degree - 2, zero + 2 * one + two + degree - 2]
    return rows


def group_of(row, sizes):
    zero, one, two = sizes
    if row < zero:
        return 0, row
    if row < zero + 2 * one:
        return 1, row - zero
    return 2, row - zero - 2 * one


class Copies:
    def __init__(self, semaphores):
        self.semaphores = semaphores
        self.count = 0

    def start(self, sources, targets):
        started = []
        for source, target in zip(sources, targets):
            copy = pltpu.make_async_copy(source, target, self.semaphores.at[self.count])
            copy.start()
            self.count += 1
            started.append(copy)
        return started


def wait(started):
    for copy in started:
        copy.wait()


def prepare_kernel(
    wigner_hbm, w_zero_hbm, w_one_hbm, w_two_hbm, radial, wide, scale, t_zero, t_one, t_two,
    wigner, w_zero, w_one, w_two, semaphores
):
    copies = Copies(semaphores)
    first = copies.start((wigner_hbm, w_zero_hbm), (wigner, w_zero))
    rest = copies.start((w_one_hbm, w_two_hbm), (w_one, w_two))
    scale[...] = radial[...].astype(F32).T
    wait(first)
    for j in range(wigner.shape[0]):
        wide[j] = wigner[j].astype(F32)
    t_zero[...] = w_zero[...].T
    wait(rest)
    for part in range(2):
        t_one[part] = w_one[part].T
        t_two[part] = w_two[part].T


def fill_spread(degree, sizes, hits, wide_ref, spread_ref):
    nodes, edges = hits.shape
    for j in range(2 * degree + 1):
        for place, k in enumerate(kept_rows(degree, sizes)):
            row = wide_ref[degree * degree + j, k : k + 1, :]
            row = jnp.broadcast_to(row, (16, edges)).astype(BF16)
            for part in range(nodes // 16):
                at = j * nodes + part * 16
                spread_ref[at : at + 16, place * edges : (place + 1) * edges] = (
                    hits[part * 16 : (part + 1) * 16] * row
                )


def turn(pieces, sizes, hits, wide_ref, spreads, stacked, degree, width):
    nodes, edges = hits.shape
    orders = 2 * degree + 1
    spread_ref = spreads[degree % 2]
    fill_spread(degree, sizes, hits, wide_ref, spread_ref)
    for j in range(orders):
        column = (degree * degree + j) * width
        at = j * nodes
        for piece in pieces:
            stacked[at : at + piece.shape[0], :] = piece[:, column : column + width]
            at += piece.shape[0]
    count = len(kept_rows(degree, sizes))
    return dot_tn(stacked[0 : orders * nodes, :], spread_ref[0 : orders * nodes, 0 : count * edges])


def nodes_kernel(sizes, order, sources, wide, scale, first, gating, *refs):
    pieces, (x_zero, x_one, x_two, scalar, gate), (even, odd, stacked) = (
        refs[:-8],
        refs[-8:-3],
        refs[-3:],
    )
    width = gating.shape[0]
    edges = sources.shape[1]
    hits = shard_hits(order, pieces[0].shape[0], sources[...])
    outs = (x_zero, x_one, x_two)
    for degree in range(sizes[0]):
        turned = turn(pieces, sizes, hits, wide, (even, odd), stacked, degree, width)
        for place, k in enumerate(kept_rows(degree, sizes)):
            group, row = group_of(k, sizes)
            outs[group][row * width : (row + 1) * width, :] = (
                turned[:, place * edges : (place + 1) * edges] * scale[...]
            ).astype(BF16)
    low = dot_nn(first[...], x_zero[...])
    scalar[...] = low
    gate[...] = jax.nn.sigmoid(dot_tn(gating[...], low.astype(BF16)))


def products_kernel(
    sizes, x_zero, x_one, x_two, scalar, gate, w_zero, w_one, w_two,
    m_zero, m_one, m_two, messages, mixed
):
    width, edges = gate.shape
    zero, one, two = sizes

    def settle(out, first_row, base, count):
        for row in range(count):
            k = base + row
            at = (first_row + row) * width
            raw = mixed[row * width : (row + 1) * width, :]
            out[at : at + width, :] = raw.astype(BF16)
            if k == 0:
                v = scalar[...]
                value = v * jax.nn.sigmoid(v)
            else:
                value = raw * gate[...]
            store_row(messages, sizes, k, value)

    mixed[0 : zero * width, :] = dot_nn(w_zero[...], x_zero[...])
    settle(m_zero, 0, 0, zero)
    base = zero
    for size, x, w, out in ((one, x_one, w_one, m_one), (two, x_two, w_two, m_two)):
        half = size * width
        mixed[0:half, :] = dot_nn(w[0], x[:half]) - dot_nn(w[1], x[half:])
        settle(out, 0, base, size)
        mixed[0:half, :] = dot_nn(w[1], x[:half]) + dot_nn(w[0], x[half:])
        settle(out, size, base + size, size)
        base += 2 * size


def store_row(values, sizes, k, value):
    edges = value.shape[1]
    for degree in range(sizes[0]):
        rows = kept_rows(degree, sizes)
        if k in rows:
            place = rows.index(k)
            values[degree, :, place * edges : (place + 1) * edges] = value.astype(BF16)


def shard_hits(order, shard, index):
    mine = lax.axis_index("graph")
    rows = lax.broadcasted_iota(jnp.int32, (shard, index.shape[1]), 0)
    hits = [(rows + (other ^ mine) * shard == index).astype(F32).astype(BF16) for other in order]
    return jnp.concatenate(hits, axis=0)


def only_live(live, index):
    slots = lax.broadcasted_iota(jnp.int32, index.shape, 1)
    return jnp.where(slots < live[0], index[...], -1)


def place_of(stages):
    mine = jnp.int32(0)
    for axis, bit in stages:
        mine = 2 * mine + jnp.where((lax.axis_index(axis) & bit) != 0, 1, 0)
    return mine


def cotangent_kernel(
    sizes, order, live, targets, wide, scalar, gate, gating, m_zero, m_one, m_two, *refs
):
    pieces, (g_zero, g_one, g_two, gate_low), (even, odd, stacked, total, head) = (
        refs[:-9],
        refs[-9:-5],
        refs[-5:],
    )
    width, edges = gate.shape
    hits = shard_hits(order, pieces[0].shape[0], only_live(live, targets))
    outs = (g_zero, g_one, g_two)
    mixed = (m_zero, m_one, m_two)
    total[...] = jnp.zeros((width, edges), F32)
    for degree in range(sizes[0]):
        turned = turn(pieces, sizes, hits, wide, (even, odd), stacked, degree, width)
        for place, k in enumerate(kept_rows(degree, sizes)):
            group, row = group_of(k, sizes)
            value = turned[:, place * edges : (place + 1) * edges]
            if k == 0:
                head[...] = value
            else:
                at = row * width
                value = value * gate[...]
                outs[group][at : at + width, :] = value.astype(BF16)
                total[...] += value * mixed[group][at : at + width, :].astype(F32)
    low = (total[...] * (1.0 - gate[...])).astype(BF16)
    gate_low[...] = low
    v = scalar[...]
    s = jax.nn.sigmoid(v)
    first = head[...] * s * (1.0 + v * (1.0 - s)) + dot_nn(gating[...], low)
    g_zero[0:width, :] = first.astype(BF16)


def runs(block, flat, rows):
    at = 0
    while at < rows:
        step = min(rows - at, block - (flat + at) % block)
        yield at, step, (flat + at) // block
        at += step


def place_rows(mine, out, block, flat, values):
    for at, step, index in runs(block, flat, values.shape[0]):
        start = pl.multiple_of(flat + at + ((index ^ mine) - index) * block, 16)
        out[pl.ds(start, step), :] = values[at : at + step]


def place_matrix(mine, out, block, flat, total, rows, columns, width):
    for column in range(0, columns, width):
        place_rows(mine, out, block, flat, total[0:rows, column : column + width].astype(BF16))
        flat += rows
    return flat


def finish_rows(mine, out, block, flat, kept, sent):
    rows, width = out.shape
    if flat < rows:
        place_rows(mine, out, block, flat, jnp.zeros((rows - flat, width), BF16))
    kept[...] = out[: rows // 2]
    sent[...] = out[rows // 2 :]


def grad_a_kernel(block, stages, x_two, g_two, x_one, g_one, kept, sent, out, total):
    mine = place_of(stages)
    width = out.shape[1]
    half = x_two.shape[0] // 2
    total[0:half, 0:half] = dot_nt(x_two[:half], g_two[:half]) + dot_nt(x_two[half:], g_two[half:])
    flat = place_matrix(mine, out, block, 0, total, half, half, width)
    total[0:half, 0:half] = dot_nt(x_two[:half], g_two[half:]) - dot_nt(x_two[half:], g_two[:half])
    flat = place_matrix(mine, out, block, flat, total, half, half, width)
    half = x_one.shape[0] // 2
    total[0:half, 0:half] = dot_nt(x_one[:half], g_one[:half]) + dot_nt(x_one[half:], g_one[half:])
    flat = place_matrix(mine, out, block, flat, total, half, half, width)
    finish_rows(mine, out, block, flat, kept, sent)


def grad_b_kernel(
    block, stages, x_one, g_one, x_zero, g_zero, scalar, gate_low, kept, sent, out, total
):
    mine = place_of(stages)
    width = out.shape[1]
    half = x_one.shape[0] // 2
    total[0:half, 0:half] = dot_nt(x_one[:half], g_one[half:]) - dot_nt(x_one[half:], g_one[:half])
    flat = place_matrix(mine, out, block, 0, total, half, half, width)
    rows = x_zero.shape[0]
    total[...] = dot_nt(x_zero[...], g_zero[...])
    flat = place_matrix(mine, out, block, flat, total, rows, rows, width)
    gate_grad = dot_nt(scalar[...].astype(BF16), gate_low[...]).astype(BF16)
    place_rows(mine, out, block, flat, gate_grad)
    finish_rows(mine, out, block, flat + width, kept, sent)


def spread_back(sizes, hits, wide, spreads, values, kept, sent):
    width = values.shape[1]
    half = kept.shape[0]
    nodes, edges = hits.shape
    for degree in range(sizes[0]):
        spread_ref = spreads[degree % 2]
        fill_spread(degree, sizes, hits, wide, spread_ref)
        lanes = len(kept_rows(degree, sizes)) * edges
        orders = 2 * degree + 1
        summed = dot_nt(
            spread_ref[0 : orders * nodes, 0:lanes], values[degree, :, 0:lanes]
        ).astype(BF16)
        for j in range(orders):
            column = (degree * degree + j) * width
            kept[:, column : column + width] = summed[j * nodes : j * nodes + half]
            sent[:, column : column + width] = summed[j * nodes + half : (j + 1) * nodes]


def back_kernel(
    sizes, order, live, w_zero_hbm, w_one_hbm, w_two_hbm, sources, targets, wide, scale, messages,
    g_zero, g_one, g_two, sum_kept, sum_sent, grad_kept, grad_sent,
    w_zero, w_one, w_two, even, odd, values, moved, semaphores
):
    copies = Copies(semaphores)
    given = copies.start((w_zero_hbm, w_one_hbm, w_two_hbm), (w_zero, w_one, w_two))
    shard = 2 * sum_kept.shape[0] // len(order)
    hits = shard_hits(order, shard, only_live(live, targets))
    spread_back(sizes, hits, wide, (even, odd), messages, sum_kept, sum_sent)

    zero, one, two = sizes
    width = scale.shape[0]

    def settle(base, count):
        for row in range(count):
            value = moved[row * width : (row + 1) * width, :] * scale[...]
            store_row(values, sizes, base + row, value)

    wait(given)
    moved[0 : zero * width, :] = dot_nn(w_zero[...], g_zero[...])
    settle(0, zero)
    base = zero
    for size, g, w in ((one, g_one, w_one), (two, g_two, w_two)):
        half = size * width
        moved[0:half, :] = dot_nn(w[0], g[:half]) + dot_nn(w[1], g[half:])
        settle(base, size)
        moved[0:half, :] = dot_nn(w[0], g[half:]) - dot_nn(w[1], g[:half])
        settle(base + size, size)
        base += 2 * size
    hits = shard_hits(order, shard, sources[...])
    spread_back(sizes, hits, wide, (even, odd), values, grad_kept, grad_sent)


def finish_kernel(sizes, block_count, block, stages_a, stages_b, high, *refs):
    if high:
        refs = refs[4:]
    rows_a, rows_b, grad_two, grad_one, grad_zero, grad_gate, wide_a, wide_b, semaphores = refs
    width = rows_a.shape[1]
    zero, one, two = sizes
    list_a = [(grad_two.at[part], two, column) for part in range(2) for column in range(two)]
    list_a += [(grad_one.at[0], one, column) for column in range(one)]
    list_b = [(grad_one.at[1], one, column) for column in range(one)]
    list_b += [(grad_zero, zero, column) for column in range(zero)] + [(grad_gate, 1, 0)]
    axis, bit = stages_a[0]
    first = jnp.where((lax.axis_index(axis) & bit) != 0, 1, 0)
    half = block_count // 2

    def write(copies, pieces, mine, rows, wide, low, high_end):
        started, flat = [], 0
        for target, size, column in pieces:
            begin, end = max(flat, low), min(flat + size * width, high_end)
            if begin < end:
                for at, step, index in runs(block, begin, end - begin):
                    place = (index ^ mine) - (half if high else 0)
                    start = pl.multiple_of(place * block + (begin + at) % block, 16)
                    to = begin + at - low
                    wide[to : to + step, :] = rows[pl.ds(start, step), :].astype(F32)
                started += copies.start(
                    (wide.at[begin - low : end - low],),
                    (
                        target.at[
                            begin - flat : end - flat, column * width : (column + 1) * width
                        ],
                    ),
                )
            flat += size * width
        return started

    for side in range(2):

        @pl.when(first == (1 - side if high else side))
        def _(side=side):
            copies = Copies(semaphores)
            low, end = side * half * block, (side + 1) * half * block
            started = write(copies, list_a, place_of(stages_a), rows_a, wide_a, low, end)
            started += write(copies, list_b, place_of(stages_b), rows_b, wide_b, low, end)
            wait(started)


SMEM = pl.BlockSpec(memory_space=pltpu.SMEM)
VMEM = pl.BlockSpec(memory_space=pltpu.VMEM)
ANY = pl.BlockSpec(memory_space=pl.ANY)


def call(
    kernel, out_shape, args, scratch=(), smem=0, hbm=0, copies=0, flops=0, moved=0, aliased=0
):
    vmem = [pltpu.with_memory_space_constraint(a, pltpu.VMEM) for a in args[smem + hbm :]]
    held = sum(math.prod(a.shape) * jnp.dtype(a.dtype).itemsize for a in scratch)
    held += held // 8
    if copies:
        scratch = [*scratch, pltpu.SemaphoreType.DMA((copies,))]
    return pl.pallas_call(
        kernel,
        out_shape=out_shape,
        in_specs=[SMEM] * smem + [ANY] * hbm + [VMEM] * len(vmem),
        out_specs=tuple(ANY if isinstance(o, jax.ShapeDtypeStruct) else VMEM for o in out_shape),
        scratch_shapes=list(scratch),
        input_output_aliases={i: i for i in range(aliased)},
        compiler_params=pltpu.CompilerParams(vmem_limit_bytes=held + SPARE_VMEM),
        cost_estimate=pl.CostEstimate(
            flops=int(flops), bytes_accessed=int(moved), transcendentals=0
        ),
    )(*args[: smem + hbm], *vmem)


def shaped(shape, dtype):
    return jax.ShapeDtypeStruct(shape, dtype)


def exchange(value, axis, bit):
    count = lax.axis_size(axis)
    return lax.ppermute(value, axis, [(i, i ^ bit) for i in range(count)])


def bits_of(axis):
    count = lax.axis_size(axis)
    return [(axis, 1 << b) for b in range(count.bit_length() - 1)]


def relative_gather(first, second, beside):
    order, held, also = [0], [first], [second]
    for place, (axis, bit) in enumerate(bits_of("graph")[::-1]):
        if place == 1:
            held[1], also[0], *beside = tied(held[1], also[0], *beside)
        held = held + [exchange(block, axis, bit) for block in (first, *held[1:])]
        also = also + [exchange(block, axis, bit) for block in also]
        order = order + [o ^ bit for o in order]
    return held, also, order, beside


def relative_sum(arrays, stages):
    for axis, bit in stages:
        half = arrays[0].shape[0] // 2
        sent = jnp.concatenate([rows[half:] for rows in arrays], axis=0)
        other = exchange(sent, axis, bit)
        arrays = [
            add_low(rows[:half], other[at * half : (at + 1) * half])
            for at, rows in enumerate(arrays)
        ]
    return arrays


def tied(*values):
    return lax.optimization_barrier(values)


def add_low(kept, other):
    return (kept.astype(F32) + other.astype(F32)).astype(BF16)


def per_device(
    nodes, sources, targets, edge_counts, wigner, radial, cotangent, w_zero, w_one, w_two, w_gate
):
    width = w_gate.shape[0]
    zero, one, two = w_zero.shape[0] // width, w_one.shape[1] // width, w_two.shape[1] // width
    sizes = (zero, one, two)
    shard = nodes.shape[1]
    node_count = shard * lax.axis_size("graph")
    edges = sources.shape[1]
    coefficients = wigner.shape[2]
    kept = wigner.shape[1]
    features = nodes.shape[2]
    live = edge_counts[0]
    rotation = jnp.transpose(wigner[0], (1, 0, 2))
    radial_rows = radial[0]

    pairs = 2 * zero - 1
    spread = [
        pltpu.VMEM(((2 * d + 1) * node_count, 5 * edges), BF16) for d in (zero - 1, zero - 2)
    ]
    if zero % 2 == 0:
        spread = spread[::-1]
    stacked = pltpu.VMEM((pairs * node_count, width), BF16)
    edge_block = pltpu.VMEM((width, edges), F32)
    turn_cost = 2 * coefficients * 5 * node_count * width * edges
    edge_flops = 2 * edges * width * width * (zero * zero + 4 * one * one + 4 * two * two)
    rows = [zero * width, 2 * one * width, 2 * two * width]
    wide_rows = [pltpu.VMEM((r, edges), BF16) for r in rows]
    values_shape = pltpu.VMEM((zero, width, 5 * edges), BF16)
    products = pltpu.VMEM((zero * width, edges), F32)
    partial_shape = pltpu.VMEM((node_count // 2, features), BF16)
    weights = [pltpu.VMEM(w.shape, BF16) for w in (w_zero, w_one, w_two)]

    prepared = call(
        prepare_kernel,
        (pltpu.VMEM(rotation.shape, F32), edge_block, *weights),
        [rotation, w_zero, w_one, w_two, radial_rows],
        [pltpu.VMEM(rotation.shape, BF16), *weights],
        hbm=4,
        copies=4,
        moved=rotation.size * 8 + edge_flops / edges,
    )
    node_blocks, upstream_blocks, order, prepared = relative_gather(
        nodes[0], cotangent[0], prepared
    )
    wide, scale, *turned = prepared
    x_zero, x_one, x_two, scalar, gate = call(
        functools.partial(nodes_kernel, sizes, order),
        (*wide_rows, edge_block, edge_block),
        [sources, wide, scale, turned[0][:width], w_gate, *node_blocks],
        [*spread, stacked],
        flops=turn_cost,
        moved=4 * sum(rows) * edges,
    )
    gate, *upstream_blocks[:2] = tied(gate, *upstream_blocks[:2])
    m_zero, m_one, m_two, messages = call(
        functools.partial(products_kernel, sizes),
        (*wide_rows, values_shape),
        [x_zero, x_one, x_two, scalar, gate, *turned],
        [products],
        flops=edge_flops,
        moved=6 * sum(rows) * edges,
    )
    g_zero, g_one, g_two, gate_low = call(
        functools.partial(cotangent_kernel, sizes, order),
        (*wide_rows, pltpu.VMEM((width, edges), BF16)),
        [live, targets, wide, scalar, gate, w_gate, m_zero, m_one, m_two]
        + upstream_blocks,
        [*spread, stacked, edge_block, edge_block],
        smem=1,
        flops=turn_cost,
        moved=4 * sum(rows) * edges,
    )

    dp_bits = bits_of("dp")
    stages_a = dp_bits + bits_of("graph")
    stages_b = dp_bits[:1] + dp_bits[1:][::-1] + bits_of("graph")
    blocks = lax.axis_size("dp") * lax.axis_size("graph")
    rows_two = 2 * two * two * width
    rows_one = one * one * width
    rows_zero = zero * zero * width
    most = max(rows_two + rows_one, rows_one + rows_zero + width)
    block = -(-most // (16 * blocks)) * 16
    half_list = pltpu.VMEM((blocks * block // 2, width), BF16)
    whole_list = pltpu.VMEM((blocks * block, width), BF16)
    side = zero * width
    square = pltpu.VMEM((side, side), F32)
    a, sent_a = call(
        functools.partial(grad_a_kernel, block, stages_a),
        (half_list, half_list),
        [x_two, g_two, x_one, g_one],
        [whole_list, square],
        flops=edge_flops / 2,
        moved=4 * blocks * block * width,
    )
    b, sent_b = call(
        functools.partial(grad_b_kernel, block, stages_b),
        (half_list, half_list),
        [x_one, g_one, x_zero, g_zero, scalar, gate_low],
        [whole_list, square],
        flops=edge_flops / 2,
        moved=4 * blocks * block * width,
    )

    graph_bits = bits_of("graph")
    last = len(dp_bits) - 1
    for place, (stage_a, stage_b) in enumerate(zip(stages_a, stages_b)):
        if place > 0:
            half = a.shape[0] // 2
            a, sent_a, b, sent_b = a[:half], a[half:], b[:half], b[half:]
        other_a, other_b = exchange(sent_a, *stage_a), exchange(sent_b, *stage_b)
        if place == 0:
            a, b = add_low(a, other_a), add_low(b, other_b)
            a, b, messages = tied(a, b, messages)
            sum_kept, sum_sent, grad_kept, grad_sent = call(
                functools.partial(back_kernel, sizes, order),
                (partial_shape,) * 4,
                [
                    live, w_zero, w_one, w_two, sources, targets, wide, scale, messages,
                    g_zero, g_one, g_two,
                ],
                [*weights, *spread, pltpu.VMEM(values_shape.shape, BF16), products],
                smem=1,
                hbm=3,
                copies=3,
                flops=edge_flops + 2 * turn_cost,
                moved=8 * sum(rows) * edges,
            )
            continue
        if place == 1:
            other_a, other_b, sum_kept, sum_sent, grad_kept, grad_sent = tied(
                other_a, other_b, sum_kept, sum_sent, grad_kept, grad_sent
            )
            sum_half = add_low(sum_kept, exchange(sum_sent, *graph_bits[0]))
        if place == last:
            other_a, other_b, sum_half = tied(other_a, other_b, sum_half)
        a, b = add_low(a, other_a), add_low(b, other_b)
    for place in range(len(stages_a))[::-1]:
        half_a = (a, exchange(a, *stages_a[place]))
        half_b = (b, exchange(b, *stages_b[place]))
        if place == last + 2:
            (low_a, high_a), (low_b, high_b) = half_a, half_b
            high_a, high_b, grad_kept, grad_sent = tied(high_a, high_b, grad_kept, grad_sent)
            half_a, half_b = (low_a, high_a), (low_b, high_b)
            grad_half = add_low(grad_kept, exchange(grad_sent, *graph_bits[0]))
        if place == last:
            (low_a, high_a), (low_b, high_b) = half_a, half_b
            high_a, high_b, sum_half, grad_half = tied(high_a, high_b, sum_half, grad_half)
            half_a, half_b = (low_a, high_a), (low_b, high_b)
            summed, grad_rows = relative_sum([sum_half, grad_half], graph_bits[1:])
        if place > 0:
            a, b = jnp.concatenate(half_a, axis=0), jnp.concatenate(half_b, axis=0)

    shapes = (
        shaped((2, two * width, two * width), F32),
        shaped((2, one * width, one * width), F32),
        shaped((side, side), F32),
        shaped((width, width), F32),
    )
    half_wide = pltpu.VMEM((blocks * block // 2, width), F32)
    grads = ()
    for high, halves in ((False, (half_a[0], half_b[0])), (True, (half_a[1], half_b[1]))):
        grads = call(
            functools.partial(finish_kernel, sizes, blocks, block, stages_a, stages_b, high),
            shapes,
            [*grads, *halves],
            [half_wide, half_wide],
            hbm=len(grads),
            aliased=len(grads),
            copies=2 * two + 2 * one + zero + 3,
            moved=6 * blocks * block * width,
        )
    grad_two, grad_one, grad_zero, grad_gate = grads
    return (summed[None], grad_rows[None], grad_zero, grad_one, grad_two, grad_gate)


def solution(mesh):
    in_specs = (
        P("dp", "graph", None),
        P("dp", "graph"),
        P("dp", "graph"),
        P("dp", "graph"),
        P("dp", None, None, "graph"),
        P("dp", "graph", None),
        P("dp", "graph", None),
        P(),
        P(),
        P(),
        P(),
    )
    out_specs = (P("dp", "graph", None), P("dp", "graph", None), P(), P(), P(), P())
    return jax.shard_map(
        per_device, mesh=mesh, in_specs=in_specs, out_specs=out_specs, check_vma=False
    )
```

```python
import functools
import math

import jax
import jax.numpy as jnp
from jax import lax
from jax.experimental import pallas as pl
from jax.experimental.pallas import tpu as pltpu
from jax.sharding import PartitionSpec as P

F32 = jnp.float32
BF16 = jnp.bfloat16
SPARE_VMEM = 8 * 1024 * 1024


def dot_nn(left, right):
    return jnp.dot(left, right, preferred_element_type=F32)


def dot_nt(left, right):
    return lax.dot_general(left, right, (((1,), (1,)), ((), ())), preferred_element_type=F32)


def dot_tn(left, right):
    return lax.dot_general(left, right, (((0,), (0,)), ((), ())), preferred_element_type=F32)


def kept_rows(degree, sizes):
    zero, one, two = sizes
    rows = [degree]
    if degree >= 1:
        rows += [zero + degree - 1, zero + one + degree - 1]
    if degree >= 2:
        rows += [zero + 2 * one + degree - 2, zero + 2 * one + two + degree - 2]
    return rows


def group_of(row, sizes):
    zero, one, two = sizes
    if row < zero:
        return 0, row
    if row < zero + 2 * one:
        return 1, row - zero
    return 2, row - zero - 2 * one


class Copies:
    def __init__(self, semaphores):
        self.semaphores = semaphores
        self.count = 0

    def start(self, sources, targets):
        started = []
        for source, target in zip(sources, targets):
            copy = pltpu.make_async_copy(source, target, self.semaphores.at[self.count])
            copy.start()
            self.count += 1
            started.append(copy)
        return started


def wait(started):
    for copy in started:
        copy.wait()


def prepare_kernel(
    wigner_hbm, w_zero_hbm, w_one_hbm, w_two_hbm, radial, wide, scale, t_zero, t_one, t_two,
    wigner, w_zero, w_one, w_two, semaphores
):
    copies = Copies(semaphores)
    first = copies.start((wigner_hbm, w_zero_hbm), (wigner, w_zero))
    rest = copies.start((w_one_hbm, w_two_hbm), (w_one, w_two))
    scale[...] = radial[...].astype(F32).T
    wait(first)
    for j in range(wigner.shape[0]):
        wide[j] = wigner[j].astype(F32)
    t_zero[...] = w_zero[...].T
    wait(rest)
    for part in range(2):
        t_one[part] = w_one[part].T
        t_two[part] = w_two[part].T


def fill_spread(degree, sizes, hits, wide_ref, spread_ref):
    nodes, edges = hits.shape
    for j in range(2 * degree + 1):
        for place, k in enumerate(kept_rows(degree, sizes)):
            row = wide_ref[degree * degree + j, k : k + 1, :]
            row = jnp.broadcast_to(row, (16, edges)).astype(BF16)
            for part in range(nodes // 16):
                at = j * nodes + part * 16
                spread_ref[at : at + 16, place * edges : (place + 1) * edges] = (
                    hits[part * 16 : (part + 1) * 16] * row
                )


def turn(pieces, sizes, hits, wide_ref, spreads, stacked, degree, width):
    nodes, edges = hits.shape
    orders = 2 * degree + 1
    spread_ref = spreads[degree % 2]
    fill_spread(degree, sizes, hits, wide_ref, spread_ref)
    for j in range(orders):
        column = (degree * degree + j) * width
        at = j * nodes
        for piece in pieces:
            stacked[at : at + piece.shape[0], :] = piece[:, column : column + width]
            at += piece.shape[0]
    count = len(kept_rows(degree, sizes))
    return dot_tn(stacked[0 : orders * nodes, :], spread_ref[0 : orders * nodes, 0 : count * edges])


def nodes_kernel(sizes, order, sources, wide, scale, first, gating, *refs):
    pieces, (x_zero, x_one, x_two, scalar, gate), (even, odd, stacked) = (
        refs[:-8],
        refs[-8:-3],
        refs[-3:],
    )
    width = gating.shape[0]
    edges = sources.shape[1]
    hits = shard_hits(order, pieces[0].shape[0], sources[...])
    outs = (x_zero, x_one, x_two)
    for degree in range(sizes[0]):
        turned = turn(pieces, sizes, hits, wide, (even, odd), stacked, degree, width)
        for place, k in enumerate(kept_rows(degree, sizes)):
            group, row = group_of(k, sizes)
            outs[group][row * width : (row + 1) * width, :] = (
                turned[:, place * edges : (place + 1) * edges] * scale[...]
            ).astype(BF16)
    low = dot_nn(first[...], x_zero[...])
    scalar[...] = low
    gate[...] = jax.nn.sigmoid(dot_tn(gating[...], low.astype(BF16)))


def products_kernel(
    sizes, x_zero, x_one, x_two, scalar, gate, w_zero, w_one, w_two,
    m_zero, m_one, m_two, messages, mixed
):
    width, edges = gate.shape
    zero, one, two = sizes

    def settle(out, first_row, base, count):
        for row in range(count):
            k = base + row
            at = (first_row + row) * width
            raw = mixed[row * width : (row + 1) * width, :]
            out[at : at + width, :] = raw.astype(BF16)
            if k == 0:
                v = scalar[...]
                value = v * jax.nn.sigmoid(v)
            else:
                value = raw * gate[...]
            store_row(messages, sizes, k, value)

    mixed[0 : zero * width, :] = dot_nn(w_zero[...], x_zero[...])
    settle(m_zero, 0, 0, zero)
    base = zero
    for size, x, w, out in ((one, x_one, w_one, m_one), (two, x_two, w_two, m_two)):
        half = size * width
        mixed[0:half, :] = dot_nn(w[0], x[:half]) - dot_nn(w[1], x[half:])
        settle(out, 0, base, size)
        mixed[0:half, :] = dot_nn(w[1], x[:half]) + dot_nn(w[0], x[half:])
        settle(out, size, base + size, size)
        base += 2 * size


def store_row(values, sizes, k, value):
    edges = value.shape[1]
    for degree in range(sizes[0]):
        rows = kept_rows(degree, sizes)
        if k in rows:
            place = rows.index(k)
            values[degree, :, place * edges : (place + 1) * edges] = value.astype(BF16)


def shard_hits(order, shard, index):
    mine = lax.axis_index("graph")
    rows = lax.broadcasted_iota(jnp.int32, (shard, index.shape[1]), 0)
    hits = [(rows + (other ^ mine) * shard == index).astype(F32).astype(BF16) for other in order]
    return jnp.concatenate(hits, axis=0)


def only_live(live, index):
    slots = lax.broadcasted_iota(jnp.int32, index.shape, 1)
    return jnp.where(slots < live[0], index[...], -1)


def place_of(stages):
    mine = jnp.int32(0)
    for axis, bit in stages:
        mine = 2 * mine + jnp.where((lax.axis_index(axis) & bit) != 0, 1, 0)
    return mine


def cotangent_kernel(
    sizes, order, live, targets, wide, scalar, gate, gating, m_zero, m_one, m_two, *refs
):
    pieces, (g_zero, g_one, g_two, gate_low), (even, odd, stacked, total, head) = (
        refs[:-9],
        refs[-9:-5],
        refs[-5:],
    )
    width, edges = gate.shape
    hits = shard_hits(order, pieces[0].shape[0], only_live(live, targets))
    outs = (g_zero, g_one, g_two)
    mixed = (m_zero, m_one, m_two)
    total[...] = jnp.zeros((width, edges), F32)
    for degree in range(sizes[0]):
        turned = turn(pieces, sizes, hits, wide, (even, odd), stacked, degree, width)
        for place, k in enumerate(kept_rows(degree, sizes)):
            group, row = group_of(k, sizes)
            value = turned[:, place * edges : (place + 1) * edges]
            if k == 0:
                head[...] = value
            else:
                at = row * width
                value = value * gate[...]
                outs[group][at : at + width, :] = value.astype(BF16)
                total[...] += value * mixed[group][at : at + width, :].astype(F32)
    low = (total[...] * (1.0 - gate[...])).astype(BF16)
    gate_low[...] = low
    v = scalar[...]
    s = jax.nn.sigmoid(v)
    first = head[...] * s * (1.0 + v * (1.0 - s)) + dot_nn(gating[...], low)
    g_zero[0:width, :] = first.astype(BF16)


def runs(block, flat, rows):
    at = 0
    while at < rows:
        step = min(rows - at, block - (flat + at) % block)
        yield at, step, (flat + at) // block
        at += step


def place_rows(mine, out, block, flat, values):
    for at, step, index in runs(block, flat, values.shape[0]):
        start = pl.multiple_of(flat + at + ((index ^ mine) - index) * block, 16)
        out[pl.ds(start, step), :] = values[at : at + step]


def place_matrix(mine, out, block, flat, total, rows, columns, width):
    for column in range(0, columns, width):
        place_rows(mine, out, block, flat, total[0:rows, column : column + width].astype(BF16))
        flat += rows
    return flat


def finish_rows(mine, out, block, flat, kept, sent):
    rows, width = out.shape
    if flat < rows:
        place_rows(mine, out, block, flat, jnp.zeros((rows - flat, width), BF16))
    kept[...] = out[: rows // 2]
    sent[...] = out[rows // 2 :]


def grad_a_kernel(block, stages, x_two, g_two, x_one, g_one, kept, sent, out, total):
    mine = place_of(stages)
    width = out.shape[1]
    half = x_two.shape[0] // 2
    total[0:half, 0:half] = dot_nt(x_two[:half], g_two[:half]) + dot_nt(x_two[half:], g_two[half:])
    flat = place_matrix(mine, out, block, 0, total, half, half, width)
    total[0:half, 0:half] = dot_nt(x_two[:half], g_two[half:]) - dot_nt(x_two[half:], g_two[:half])
    flat = place_matrix(mine, out, block, flat, total, half, half, width)
    half = x_one.shape[0] // 2
    total[0:half, 0:half] = dot_nt(x_one[:half], g_one[:half]) + dot_nt(x_one[half:], g_one[half:])
    flat = place_matrix(mine, out, block, flat, total, half, half, width)
    finish_rows(mine, out, block, flat, kept, sent)


def grad_b_kernel(
    block, stages, x_one, g_one, x_zero, g_zero, scalar, gate_low, kept, sent, out, total
):
    mine = place_of(stages)
    width = out.shape[1]
    half = x_one.shape[0] // 2
    total[0:half, 0:half] = dot_nt(x_one[:half], g_one[half:]) - dot_nt(x_one[half:], g_one[:half])
    flat = place_matrix(mine, out, block, 0, total, half, half, width)
    rows = x_zero.shape[0]
    total[...] = dot_nt(x_zero[...], g_zero[...])
    flat = place_matrix(mine, out, block, flat, total, rows, rows, width)
    gate_grad = dot_nt(scalar[...].astype(BF16), gate_low[...]).astype(BF16)
    place_rows(mine, out, block, flat, gate_grad)
    finish_rows(mine, out, block, flat + width, kept, sent)


def spread_back(sizes, hits, wide, spreads, values, kept, sent):
    width = values.shape[1]
    half = kept.shape[0]
    nodes, edges = hits.shape
    for degree in range(sizes[0]):
        spread_ref = spreads[degree % 2]
        fill_spread(degree, sizes, hits, wide, spread_ref)
        lanes = len(kept_rows(degree, sizes)) * edges
        orders = 2 * degree + 1
        summed = dot_nt(
            spread_ref[0 : orders * nodes, 0:lanes], values[degree, :, 0:lanes]
        ).astype(BF16)
        for j in range(orders):
            column = (degree * degree + j) * width
            kept[:, column : column + width] = summed[j * nodes : j * nodes + half]
            sent[:, column : column + width] = summed[j * nodes + half : (j + 1) * nodes]


def back_kernel(
    sizes, order, live, w_zero_hbm, w_one_hbm, w_two_hbm, sources, targets, wide, scale, messages,
    g_zero, g_one, g_two, sum_kept, sum_sent, grad_kept, grad_sent,
    w_zero, w_one, w_two, even, odd, values, moved, semaphores
):
    copies = Copies(semaphores)
    given = copies.start((w_zero_hbm, w_one_hbm, w_two_hbm), (w_zero, w_one, w_two))
    shard = 2 * sum_kept.shape[0] // len(order)
    hits = shard_hits(order, shard, only_live(live, targets))
    spread_back(sizes, hits, wide, (even, odd), messages, sum_kept, sum_sent)

    zero, one, two = sizes
    width = scale.shape[0]

    def settle(base, count):
        for row in range(count):
            value = moved[row * width : (row + 1) * width, :] * scale[...]
            store_row(values, sizes, base + row, value)

    wait(given)
    moved[0 : zero * width, :] = dot_nn(w_zero[...], g_zero[...])
    settle(0, zero)
    base = zero
    for size, g, w in ((one, g_one, w_one), (two, g_two, w_two)):
        half = size * width
        moved[0:half, :] = dot_nn(w[0], g[:half]) + dot_nn(w[1], g[half:])
        settle(base, size)
        moved[0:half, :] = dot_nn(w[0], g[half:]) - dot_nn(w[1], g[:half])
        settle(base + size, size)
        base += 2 * size
    hits = shard_hits(order, shard, sources[...])
    spread_back(sizes, hits, wide, (even, odd), values, grad_kept, grad_sent)


def finish_kernel(sizes, block_count, block, stages_a, stages_b, high, *refs):
    if high:
        refs = refs[4:]
    rows_a, rows_b, grad_two, grad_one, grad_zero, grad_gate, wide_a, wide_b, semaphores = refs
    width = rows_a.shape[1]
    zero, one, two = sizes
    list_a = [(grad_two.at[part], two, column) for part in range(2) for column in range(two)]
    list_a += [(grad_one.at[0], one, column) for column in range(one)]
    list_b = [(grad_one.at[1], one, column) for column in range(one)]
    list_b += [(grad_zero, zero, column) for column in range(zero)] + [(grad_gate, 1, 0)]
    axis, bit = stages_a[0]
    first = jnp.where((lax.axis_index(axis) & bit) != 0, 1, 0)
    half = block_count // 2

    def write(copies, pieces, mine, rows, wide, low, high_end):
        started, flat = [], 0
        for target, size, column in pieces:
            begin, end = max(flat, low), min(flat + size * width, high_end)
            if begin < end:
                for at, step, index in runs(block, begin, end - begin):
                    place = (index ^ mine) - (half if high else 0)
                    start = pl.multiple_of(place * block + (begin + at) % block, 16)
                    to = begin + at - low
                    wide[to : to + step, :] = rows[pl.ds(start, step), :].astype(F32)
                started += copies.start(
                    (wide.at[begin - low : end - low],),
                    (
                        target.at[
                            begin - flat : end - flat, column * width : (column + 1) * width
                        ],
                    ),
                )
            flat += size * width
        return started

    for side in range(2):

        @pl.when(first == (1 - side if high else side))
        def _(side=side):
            copies = Copies(semaphores)
            low, end = side * half * block, (side + 1) * half * block
            started = write(copies, list_a, place_of(stages_a), rows_a, wide_a, low, end)
            started += write(copies, list_b, place_of(stages_b), rows_b, wide_b, low, end)
            wait(started)


SMEM = pl.BlockSpec(memory_space=pltpu.SMEM)
VMEM = pl.BlockSpec(memory_space=pltpu.VMEM)
ANY = pl.BlockSpec(memory_space=pl.ANY)


def call(
    kernel, out_shape, args, scratch=(), smem=0, hbm=0, copies=0, flops=0, moved=0, aliased=0
):
    vmem = [pltpu.with_memory_space_constraint(a, pltpu.VMEM) for a in args[smem + hbm :]]
    held = sum(math.prod(a.shape) * jnp.dtype(a.dtype).itemsize for a in scratch)
    held += held // 8
    if copies:
        scratch = [*scratch, pltpu.SemaphoreType.DMA((copies,))]
    return pl.pallas_call(
        kernel,
        out_shape=out_shape,
        in_specs=[SMEM] * smem + [ANY] * hbm + [VMEM] * len(vmem),
        out_specs=tuple(ANY if isinstance(o, jax.ShapeDtypeStruct) else VMEM for o in out_shape),
        scratch_shapes=list(scratch),
        input_output_aliases={i: i for i in range(aliased)},
        compiler_params=pltpu.CompilerParams(vmem_limit_bytes=held + SPARE_VMEM),
        cost_estimate=pl.CostEstimate(
            flops=int(flops), bytes_accessed=int(moved), transcendentals=0
        ),
    )(*args[: smem + hbm], *vmem)


def shaped(shape, dtype):
    return jax.ShapeDtypeStruct(shape, dtype)


def exchange(value, axis, bit):
    count = lax.axis_size(axis)
    return lax.ppermute(value, axis, [(i, i ^ bit) for i in range(count)])


def bits_of(axis):
    count = lax.axis_size(axis)
    return [(axis, 1 << b) for b in range(count.bit_length() - 1)]


def relative_gather(first, second, beside):
    order, held, also = [0], [first], [second]
    for place, (axis, bit) in enumerate(bits_of("graph")[::-1]):
        if place == 1:
            held[1], also[0], *beside = tied(held[1], also[0], *beside)
        held = held + [exchange(block, axis, bit) for block in (first, *held[1:])]
        also = also + [exchange(block, axis, bit) for block in also]
        order = order + [o ^ bit for o in order]
    return held, also, order, beside


def relative_sum(arrays, stages):
    for axis, bit in stages:
        half = arrays[0].shape[0] // 2
        sent = jnp.concatenate([rows[half:] for rows in arrays], axis=0)
        other = exchange(sent, axis, bit)
        arrays = [
            add_low(rows[:half], other[at * half : (at + 1) * half])
            for at, rows in enumerate(arrays)
        ]
    return arrays


def tied(*values):
    return lax.optimization_barrier(values)


def add_low(kept, other):
    return (kept.astype(F32) + other.astype(F32)).astype(BF16)


def per_device(
    nodes, sources, targets, edge_counts, wigner, radial, cotangent, w_zero, w_one, w_two, w_gate
):
    width = w_gate.shape[0]
    zero, one, two = w_zero.shape[0] // width, w_one.shape[1] // width, w_two.shape[1] // width
    sizes = (zero, one, two)
    shard = nodes.shape[1]
    node_count = shard * lax.axis_size("graph")
    edges = sources.shape[1]
    coefficients = wigner.shape[2]
    kept = wigner.shape[1]
    features = nodes.shape[2]
    live = edge_counts[0]
    rotation = jnp.transpose(wigner[0], (1, 0, 2))
    radial_rows = radial[0]

    pairs = 2 * zero - 1
    spread = [
        pltpu.VMEM(((2 * d + 1) * node_count, 5 * edges), BF16) for d in (zero - 1, zero - 2)
    ]
    if zero % 2 == 0:
        spread = spread[::-1]
    stacked = pltpu.VMEM((pairs * node_count, width), BF16)
    edge_block = pltpu.VMEM((width, edges), F32)
    turn_cost = 2 * coefficients * 5 * node_count * width * edges
    edge_flops = 2 * edges * width * width * (zero * zero + 4 * one * one + 4 * two * two)
    rows = [zero * width, 2 * one * width, 2 * two * width]
    wide_rows = [pltpu.VMEM((r, edges), BF16) for r in rows]
    values_shape = pltpu.VMEM((zero, width, 5 * edges), BF16)
    products = pltpu.VMEM((zero * width, edges), F32)
    partial_shape = pltpu.VMEM((node_count // 2, features), BF16)
    weights = [pltpu.VMEM(w.shape, BF16) for w in (w_zero, w_one, w_two)]

    prepared = call(
        prepare_kernel,
        (pltpu.VMEM(rotation.shape, F32), edge_block, *weights),
        [rotation, w_zero, w_one, w_two, radial_rows],
        [pltpu.VMEM(rotation.shape, BF16), *weights],
        hbm=4,
        copies=4,
        moved=rotation.size * 8 + edge_flops / edges,
    )
    node_blocks, upstream_blocks, order, prepared = relative_gather(
        nodes[0], cotangent[0], prepared
    )
    wide, scale, *turned = prepared
    x_zero, x_one, x_two, scalar, gate = call(
        functools.partial(nodes_kernel, sizes, order),
        (*wide_rows, edge_block, edge_block),
        [sources, wide, scale, turned[0][:width], w_gate, *node_blocks],
        [*spread, stacked],
        flops=turn_cost,
        moved=4 * sum(rows) * edges,
    )
    gate, *upstream_blocks[:2] = tied(gate, *upstream_blocks[:2])
    m_zero, m_one, m_two, messages = call(
        functools.partial(products_kernel, sizes),
        (*wide_rows, values_shape),
        [x_zero, x_one, x_two, scalar, gate, *turned],
        [products],
        flops=edge_flops,
        moved=6 * sum(rows) * edges,
    )
    g_zero, g_one, g_two, gate_low = call(
        functools.partial(cotangent_kernel, sizes, order),
        (*wide_rows, pltpu.VMEM((width, edges), BF16)),
        [live, targets, wide, scalar, gate, w_gate, m_zero, m_one, m_two]
        + upstream_blocks,
        [*spread, stacked, edge_block, edge_block],
        smem=1,
        flops=turn_cost,
        moved=4 * sum(rows) * edges,
    )

    dp_bits = bits_of("dp")
    stages_a = dp_bits + bits_of("graph")
    stages_b = dp_bits[:1] + dp_bits[1:][::-1] + bits_of("graph")[::-1]
    blocks = lax.axis_size("dp") * lax.axis_size("graph")
    rows_two = 2 * two * two * width
    rows_one = one * one * width
    rows_zero = zero * zero * width
    most = max(rows_two + rows_one, rows_one + rows_zero + width)
    block = -(-most // (16 * blocks)) * 16
    half_list = pltpu.VMEM((blocks * block // 2, width), BF16)
    whole_list = pltpu.VMEM((blocks * block, width), BF16)
    side = zero * width
    square = pltpu.VMEM((side, side), F32)
    a, sent_a = call(
        functools.partial(grad_a_kernel, block, stages_a),
        (half_list, half_list),
        [x_two, g_two, x_one, g_one],
        [whole_list, square],
        flops=edge_flops / 2,
        moved=4 * blocks * block * width,
    )
    b, sent_b = call(
        functools.partial(grad_b_kernel, block, stages_b),
        (half_list, half_list),
        [x_one, g_one, x_zero, g_zero, scalar, gate_low],
        [whole_list, square],
        flops=edge_flops / 2,
        moved=4 * blocks * block * width,
    )

    graph_bits = bits_of("graph")
    last = len(dp_bits) - 1
    for place, (stage_a, stage_b) in enumerate(zip(stages_a, stages_b)):
        if place > 0:
            half = a.shape[0] // 2
            a, sent_a, b, sent_b = a[:half], a[half:], b[:half], b[half:]
        other_a, other_b = exchange(sent_a, *stage_a), exchange(sent_b, *stage_b)
        if place == 0:
            a, b = add_low(a, other_a), add_low(b, other_b)
            b, messages = tied(b, messages)
            sum_kept, sum_sent, grad_kept, grad_sent = call(
                functools.partial(back_kernel, sizes, order),
                (partial_shape,) * 4,
                [
                    live, w_zero, w_one, w_two, sources, targets, wide, scale, messages,
                    g_zero, g_one, g_two,
                ],
                [*weights, *spread, pltpu.VMEM(values_shape.shape, BF16), products],
                smem=1,
                hbm=3,
                copies=3,
                flops=edge_flops + 2 * turn_cost,
                moved=8 * sum(rows) * edges,
            )
            continue
        if place == 1:
            other_a, other_b, sum_kept, sum_sent, grad_kept, grad_sent = tied(
                other_a, other_b, sum_kept, sum_sent, grad_kept, grad_sent
            )
            sum_half = add_low(sum_kept, exchange(sum_sent, *graph_bits[0]))
        if place == last:
            other_a, other_b, sum_half = tied(other_a, other_b, sum_half)
        a, b = add_low(a, other_a), add_low(b, other_b)
    for place in range(len(stages_a))[::-1]:
        half_a = (a, exchange(a, *stages_a[place]))
        half_b = (b, exchange(b, *stages_b[place]))
        if place == last + 2:
            (low_a, high_a), (low_b, high_b) = half_a, half_b
            high_b, grad_kept, grad_sent = tied(high_b, grad_kept, grad_sent)
            half_a, half_b = (low_a, high_a), (low_b, high_b)
            grad_half = add_low(grad_kept, exchange(grad_sent, *graph_bits[0]))
        if place == last:
            (low_a, high_a), (low_b, high_b) = half_a, half_b
            high_a, sum_half, grad_half = tied(high_a, sum_half, grad_half)
            half_a, half_b = (low_a, high_a), (low_b, high_b)
            summed, grad_rows = relative_sum([sum_half, grad_half], graph_bits[1:])
        if place > 0:
            a, b = jnp.concatenate(half_a, axis=0), jnp.concatenate(half_b, axis=0)

    shapes = (
        shaped((2, two * width, two * width), F32),
        shaped((2, one * width, one * width), F32),
        shaped((side, side), F32),
        shaped((width, width), F32),
    )
    half_wide = pltpu.VMEM((blocks * block // 2, width), F32)
    grads = ()
    for high, halves in ((False, (half_a[0], half_b[0])), (True, (half_a[1], half_b[1]))):
        grads = call(
            functools.partial(finish_kernel, sizes, blocks, block, stages_a, stages_b, high),
            shapes,
            [*grads, *halves],
            [half_wide, half_wide],
            hbm=len(grads),
            aliased=len(grads),
            copies=2 * two + 2 * one + zero + 3,
            moved=6 * blocks * block * width,
        )
    grad_two, grad_one, grad_zero, grad_gate = grads
    return (summed[None], grad_rows[None], grad_zero, grad_one, grad_two, grad_gate)


def solution(mesh):
    in_specs = (
        P("dp", "graph", None),
        P("dp", "graph"),
        P("dp", "graph"),
        P("dp", "graph"),
        P("dp", None, None, "graph"),
        P("dp", "graph", None),
        P("dp", "graph", None),
        P(),
        P(),
        P(),
        P(),
    )
    out_specs = (P("dp", "graph", None), P("dp", "graph", None), P(), P(), P(), P())
    return jax.shard_map(
        per_device, mesh=mesh, in_specs=in_specs, out_specs=out_specs, check_vma=False
    )
```

```python
import functools
import math

import jax
import jax.numpy as jnp
from jax import lax
from jax.experimental import pallas as pl
from jax.experimental.pallas import tpu as pltpu
from jax.sharding import PartitionSpec as P

F32 = jnp.float32
BF16 = jnp.bfloat16
SPARE_VMEM = 8 * 1024 * 1024


def dot_nn(left, right):
    return jnp.dot(left, right, preferred_element_type=F32)


def dot_nt(left, right):
    return lax.dot_general(left, right, (((1,), (1,)), ((), ())), preferred_element_type=F32)


def dot_tn(left, right):
    return lax.dot_general(left, right, (((0,), (0,)), ((), ())), preferred_element_type=F32)


def kept_rows(degree, sizes):
    zero, one, two = sizes
    rows = [degree]
    if degree >= 1:
        rows += [zero + degree - 1, zero + one + degree - 1]
    if degree >= 2:
        rows += [zero + 2 * one + degree - 2, zero + 2 * one + two + degree - 2]
    return rows


def group_of(row, sizes):
    zero, one, two = sizes
    if row < zero:
        return 0, row
    if row < zero + 2 * one:
        return 1, row - zero
    return 2, row - zero - 2 * one


class Copies:
    def __init__(self, semaphores):
        self.semaphores = semaphores
        self.count = 0

    def start(self, sources, targets):
        started = []
        for source, target in zip(sources, targets):
            copy = pltpu.make_async_copy(source, target, self.semaphores.at[self.count])
            copy.start()
            self.count += 1
            started.append(copy)
        return started


def wait(started):
    for copy in started:
        copy.wait()


def prepare_kernel(
    wigner_hbm, w_zero_hbm, w_one_hbm, w_two_hbm, radial, wide, scale, t_zero, t_one, t_two,
    wigner, w_zero, w_one, w_two, semaphores
):
    copies = Copies(semaphores)
    first = copies.start((wigner_hbm, w_zero_hbm), (wigner, w_zero))
    rest = copies.start((w_one_hbm, w_two_hbm), (w_one, w_two))
    scale[...] = radial[...].astype(F32).T
    wait(first)
    for j in range(wigner.shape[0]):
        wide[j] = wigner[j].astype(F32)
    t_zero[...] = w_zero[...].T
    wait(rest)
    for part in range(2):
        t_one[part] = w_one[part].T
        t_two[part] = w_two[part].T


def fill_spread(degree, sizes, hits, wide_ref, spread_ref):
    nodes, edges = hits.shape
    for j in range(2 * degree + 1):
        for place, k in enumerate(kept_rows(degree, sizes)):
            row = wide_ref[degree * degree + j, k : k + 1, :]
            row = jnp.broadcast_to(row, (16, edges)).astype(BF16)
            for part in range(nodes // 16):
                at = j * nodes + part * 16
                spread_ref[at : at + 16, place * edges : (place + 1) * edges] = (
                    hits[part * 16 : (part + 1) * 16] * row
                )


def turn(pieces, sizes, hits, wide_ref, spreads, stacked, degree, width):
    nodes, edges = hits.shape
    orders = 2 * degree + 1
    spread_ref = spreads[degree % 2]
    fill_spread(degree, sizes, hits, wide_ref, spread_ref)
    for j in range(orders):
        column = (degree * degree + j) * width
        at = j * nodes
        for piece in pieces:
            stacked[at : at + piece.shape[0], :] = piece[:, column : column + width]
            at += piece.shape[0]
    count = len(kept_rows(degree, sizes))
    return dot_tn(stacked[0 : orders * nodes, :], spread_ref[0 : orders * nodes, 0 : count * edges])


def nodes_kernel(sizes, order, sources, wide, scale, first, gating, *refs):
    pieces, (x_zero, x_one, x_two, scalar, gate), (even, odd, stacked) = (
        refs[:-8],
        refs[-8:-3],
        refs[-3:],
    )
    width = gating.shape[0]
    edges = sources.shape[1]
    hits = shard_hits(order, pieces[0].shape[0], sources[...])
    outs = (x_zero, x_one, x_two)
    for degree in range(sizes[0]):
        turned = turn(pieces, sizes, hits, wide, (even, odd), stacked, degree, width)
        for place, k in enumerate(kept_rows(degree, sizes)):
            group, row = group_of(k, sizes)
            outs[group][row * width : (row + 1) * width, :] = (
                turned[:, place * edges : (place + 1) * edges] * scale[...]
            ).astype(BF16)
    low = dot_nn(first[...], x_zero[...])
    scalar[...] = low
    gate[...] = jax.nn.sigmoid(dot_tn(gating[...], low.astype(BF16)))


def products_kernel(
    sizes, x_zero, x_one, x_two, scalar, gate, w_zero, w_one, w_two,
    m_zero, m_one, m_two, messages, mixed
):
    width, edges = gate.shape
    zero, one, two = sizes

    def settle(out, first_row, base, count):
        for row in range(count):
            k = base + row
            at = (first_row + row) * width
            raw = mixed[row * width : (row + 1) * width, :]
            out[at : at + width, :] = raw.astype(BF16)
            if k == 0:
                v = scalar[...]
                value = v * jax.nn.sigmoid(v)
            else:
                value = raw * gate[...]
            store_row(messages, sizes, k, value)

    mixed[0 : zero * width, :] = dot_nn(w_zero[...], x_zero[...])
    settle(m_zero, 0, 0, zero)
    base = zero
    for size, x, w, out in ((one, x_one, w_one, m_one), (two, x_two, w_two, m_two)):
        half = size * width
        mixed[0:half, :] = dot_nn(w[0], x[:half]) - dot_nn(w[1], x[half:])
        settle(out, 0, base, size)
        mixed[0:half, :] = dot_nn(w[1], x[:half]) + dot_nn(w[0], x[half:])
        settle(out, size, base + size, size)
        base += 2 * size


def store_row(values, sizes, k, value):
    edges = value.shape[1]
    for degree in range(sizes[0]):
        rows = kept_rows(degree, sizes)
        if k in rows:
            place = rows.index(k)
            values[degree, :, place * edges : (place + 1) * edges] = value.astype(BF16)


def shard_hits(order, shard, index):
    mine = lax.axis_index("graph")
    rows = lax.broadcasted_iota(jnp.int32, (shard, index.shape[1]), 0)
    hits = [(rows + (other ^ mine) * shard == index).astype(F32).astype(BF16) for other in order]
    return jnp.concatenate(hits, axis=0)


def only_live(live, index):
    slots = lax.broadcasted_iota(jnp.int32, index.shape, 1)
    return jnp.where(slots < live[0], index[...], -1)


def place_of(stages):
    mine = jnp.int32(0)
    for axis, bit in stages:
        mine = 2 * mine + jnp.where((lax.axis_index(axis) & bit) != 0, 1, 0)
    return mine


def cotangent_kernel(
    sizes, order, live, targets, wide, scalar, gate, gating, m_zero, m_one, m_two, *refs
):
    pieces, (g_zero, g_one, g_two, gate_low), (even, odd, stacked, total, head) = (
        refs[:-9],
        refs[-9:-5],
        refs[-5:],
    )
    width, edges = gate.shape
    hits = shard_hits(order, pieces[0].shape[0], only_live(live, targets))
    outs = (g_zero, g_one, g_two)
    mixed = (m_zero, m_one, m_two)
    total[...] = jnp.zeros((width, edges), F32)
    for degree in range(sizes[0]):
        turned = turn(pieces, sizes, hits, wide, (even, odd), stacked, degree, width)
        for place, k in enumerate(kept_rows(degree, sizes)):
            group, row = group_of(k, sizes)
            value = turned[:, place * edges : (place + 1) * edges]
            if k == 0:
                head[...] = value
            else:
                at = row * width
                value = value * gate[...]
                outs[group][at : at + width, :] = value.astype(BF16)
                total[...] += value * mixed[group][at : at + width, :].astype(F32)
    low = (total[...] * (1.0 - gate[...])).astype(BF16)
    gate_low[...] = low
    v = scalar[...]
    s = jax.nn.sigmoid(v)
    first = head[...] * s * (1.0 + v * (1.0 - s)) + dot_nn(gating[...], low)
    g_zero[0:width, :] = first.astype(BF16)


def runs(block, flat, rows):
    at = 0
    while at < rows:
        step = min(rows - at, block - (flat + at) % block)
        yield at, step, (flat + at) // block
        at += step


def place_rows(mine, out, block, flat, values):
    for at, step, index in runs(block, flat, values.shape[0]):
        start = pl.multiple_of(flat + at + ((index ^ mine) - index) * block, 16)
        out[pl.ds(start, step), :] = values[at : at + step]


def place_matrix(mine, out, block, flat, total, rows, columns, width):
    for column in range(0, columns, width):
        place_rows(mine, out, block, flat, total[0:rows, column : column + width].astype(BF16))
        flat += rows
    return flat


def finish_rows(mine, out, block, flat, kept, sent):
    rows, width = out.shape
    if flat < rows:
        place_rows(mine, out, block, flat, jnp.zeros((rows - flat, width), BF16))
    kept[...] = out[: rows // 2]
    sent[...] = out[rows // 2 :]


def grad_a_kernel(block, stages, x_two, g_two, x_one, g_one, kept, sent, out, total):
    mine = place_of(stages)
    width = out.shape[1]
    half = x_two.shape[0] // 2
    total[0:half, 0:half] = dot_nt(x_two[:half], g_two[:half]) + dot_nt(x_two[half:], g_two[half:])
    flat = place_matrix(mine, out, block, 0, total, half, half, width)
    total[0:half, 0:half] = dot_nt(x_two[:half], g_two[half:]) - dot_nt(x_two[half:], g_two[:half])
    flat = place_matrix(mine, out, block, flat, total, half, half, width)
    half = x_one.shape[0] // 2
    total[0:half, 0:half] = dot_nt(x_one[:half], g_one[:half]) + dot_nt(x_one[half:], g_one[half:])
    flat = place_matrix(mine, out, block, flat, total, half, half, width)
    finish_rows(mine, out, block, flat, kept, sent)


def grad_b_kernel(
    block, stages, x_one, g_one, x_zero, g_zero, scalar, gate_low, kept, sent, out, total
):
    mine = place_of(stages)
    width = out.shape[1]
    half = x_one.shape[0] // 2
    total[0:half, 0:half] = dot_nt(x_one[:half], g_one[half:]) - dot_nt(x_one[half:], g_one[:half])
    flat = place_matrix(mine, out, block, 0, total, half, half, width)
    rows = x_zero.shape[0]
    total[...] = dot_nt(x_zero[...], g_zero[...])
    flat = place_matrix(mine, out, block, flat, total, rows, rows, width)
    gate_grad = dot_nt(scalar[...].astype(BF16), gate_low[...]).astype(BF16)
    place_rows(mine, out, block, flat, gate_grad)
    finish_rows(mine, out, block, flat + width, kept, sent)


def spread_back(sizes, hits, wide, spreads, values, kept, sent):
    width = values.shape[1]
    half = kept.shape[0]
    nodes, edges = hits.shape
    for degree in range(sizes[0]):
        spread_ref = spreads[degree % 2]
        fill_spread(degree, sizes, hits, wide, spread_ref)
        lanes = len(kept_rows(degree, sizes)) * edges
        orders = 2 * degree + 1
        summed = dot_nt(
            spread_ref[0 : orders * nodes, 0:lanes], values[degree, :, 0:lanes]
        ).astype(BF16)
        for j in range(orders):
            column = (degree * degree + j) * width
            kept[:, column : column + width] = summed[j * nodes : j * nodes + half]
            sent[:, column : column + width] = summed[j * nodes + half : (j + 1) * nodes]


def back_kernel(
    sizes, order, live, w_zero_hbm, w_one_hbm, w_two_hbm, sources, targets, wide, scale, messages,
    g_zero, g_one, g_two, sum_kept, sum_sent, grad_kept, grad_sent,
    w_zero, w_one, w_two, even, odd, values, moved, semaphores
):
    copies = Copies(semaphores)
    given = copies.start((w_zero_hbm, w_one_hbm, w_two_hbm), (w_zero, w_one, w_two))
    shard = 2 * sum_kept.shape[0] // len(order)
    hits = shard_hits(order, shard, only_live(live, targets))
    spread_back(sizes, hits, wide, (even, odd), messages, sum_kept, sum_sent)

    zero, one, two = sizes
    width = scale.shape[0]

    def settle(base, count):
        for row in range(count):
            value = moved[row * width : (row + 1) * width, :] * scale[...]
            store_row(values, sizes, base + row, value)

    wait(given)
    moved[0 : zero * width, :] = dot_nn(w_zero[...], g_zero[...])
    settle(0, zero)
    base = zero
    for size, g, w in ((one, g_one, w_one), (two, g_two, w_two)):
        half = size * width
        moved[0:half, :] = dot_nn(w[0], g[:half]) + dot_nn(w[1], g[half:])
        settle(base, size)
        moved[0:half, :] = dot_nn(w[0], g[half:]) - dot_nn(w[1], g[:half])
        settle(base + size, size)
        base += 2 * size
    hits = shard_hits(order, shard, sources[...])
    spread_back(sizes, hits, wide, (even, odd), values, grad_kept, grad_sent)


def finish_kernel(sizes, block_count, block, stages_a, stages_b, high, *refs):
    if high:
        refs = refs[4:]
    rows_a, rows_b, grad_two, grad_one, grad_zero, grad_gate, wide_a, wide_b, semaphores = refs
    width = rows_a.shape[1]
    zero, one, two = sizes
    list_a = [(grad_two.at[part], two, column) for part in range(2) for column in range(two)]
    list_a += [(grad_one.at[0], one, column) for column in range(one)]
    list_b = [(grad_one.at[1], one, column) for column in range(one)]
    list_b += [(grad_zero, zero, column) for column in range(zero)] + [(grad_gate, 1, 0)]
    axis, bit = stages_a[0]
    first = jnp.where((lax.axis_index(axis) & bit) != 0, 1, 0)
    half = block_count // 2

    def write(copies, pieces, mine, rows, wide, low, high_end):
        started, flat = [], 0
        for target, size, column in pieces:
            begin, end = max(flat, low), min(flat + size * width, high_end)
            if begin < end:
                for at, step, index in runs(block, begin, end - begin):
                    place = (index ^ mine) - (half if high else 0)
                    start = pl.multiple_of(place * block + (begin + at) % block, 16)
                    to = begin + at - low
                    wide[to : to + step, :] = rows[pl.ds(start, step), :].astype(F32)
                started += copies.start(
                    (wide.at[begin - low : end - low],),
                    (
                        target.at[
                            begin - flat : end - flat, column * width : (column + 1) * width
                        ],
                    ),
                )
            flat += size * width
        return started

    for side in range(2):

        @pl.when(first == (1 - side if high else side))
        def _(side=side):
            copies = Copies(semaphores)
            low, end = side * half * block, (side + 1) * half * block
            started = write(copies, list_a, place_of(stages_a), rows_a, wide_a, low, end)
            started += write(copies, list_b, place_of(stages_b), rows_b, wide_b, low, end)
            wait(started)


SMEM = pl.BlockSpec(memory_space=pltpu.SMEM)
VMEM = pl.BlockSpec(memory_space=pltpu.VMEM)
ANY = pl.BlockSpec(memory_space=pl.ANY)


def call(
    kernel, out_shape, args, scratch=(), smem=0, hbm=0, copies=0, flops=0, moved=0, aliased=0
):
    vmem = [pltpu.with_memory_space_constraint(a, pltpu.VMEM) for a in args[smem + hbm :]]
    held = sum(math.prod(a.shape) * jnp.dtype(a.dtype).itemsize for a in scratch)
    held += held // 8
    if copies:
        scratch = [*scratch, pltpu.SemaphoreType.DMA((copies,))]
    return pl.pallas_call(
        kernel,
        out_shape=out_shape,
        in_specs=[SMEM] * smem + [ANY] * hbm + [VMEM] * len(vmem),
        out_specs=tuple(ANY if isinstance(o, jax.ShapeDtypeStruct) else VMEM for o in out_shape),
        scratch_shapes=list(scratch),
        input_output_aliases={i: i for i in range(aliased)},
        compiler_params=pltpu.CompilerParams(vmem_limit_bytes=held + SPARE_VMEM),
        cost_estimate=pl.CostEstimate(
            flops=int(flops), bytes_accessed=int(moved), transcendentals=0
        ),
    )(*args[: smem + hbm], *vmem)


def shaped(shape, dtype):
    return jax.ShapeDtypeStruct(shape, dtype)


def exchange(value, axis, bit):
    count = lax.axis_size(axis)
    return lax.ppermute(value, axis, [(i, i ^ bit) for i in range(count)])


def bits_of(axis):
    count = lax.axis_size(axis)
    return [(axis, 1 << b) for b in range(count.bit_length() - 1)]


def relative_gather(first, second, beside):
    order, held, also = [0], [first], [second]
    for place, (axis, bit) in enumerate(bits_of("graph")[::-1]):
        if place == 1:
            held[1], also[0], *beside = tied(held[1], also[0], *beside)
        held = held + [exchange(block, axis, bit) for block in (first, *held[1:])]
        also = also + [exchange(block, axis, bit) for block in also]
        order = order + [o ^ bit for o in order]
    return held, also, order, beside


def relative_sum(arrays, stages):
    for axis, bit in stages:
        half = arrays[0].shape[0] // 2
        sent = jnp.concatenate([rows[half:] for rows in arrays], axis=0)
        other = exchange(sent, axis, bit)
        arrays = [
            add_low(rows[:half], other[at * half : (at + 1) * half])
            for at, rows in enumerate(arrays)
        ]
    return arrays


def tied(*values):
    return lax.optimization_barrier(values)


def add_low(kept, other):
    return (kept.astype(F32) + other.astype(F32)).astype(BF16)


def per_device(
    nodes, sources, targets, edge_counts, wigner, radial, cotangent, w_zero, w_one, w_two, w_gate
):
    width = w_gate.shape[0]
    zero, one, two = w_zero.shape[0] // width, w_one.shape[1] // width, w_two.shape[1] // width
    sizes = (zero, one, two)
    shard = nodes.shape[1]
    node_count = shard * lax.axis_size("graph")
    edges = sources.shape[1]
    coefficients = wigner.shape[2]
    kept = wigner.shape[1]
    features = nodes.shape[2]
    live = edge_counts[0]
    rotation = jnp.transpose(wigner[0], (1, 0, 2))
    radial_rows = radial[0]

    pairs = 2 * zero - 1
    spread = [
        pltpu.VMEM(((2 * d + 1) * node_count, 5 * edges), BF16) for d in (zero - 1, zero - 2)
    ]
    if zero % 2 == 0:
        spread = spread[::-1]
    stacked = pltpu.VMEM((pairs * node_count, width), BF16)
    edge_block = pltpu.VMEM((width, edges), F32)
    turn_cost = 2 * coefficients * 5 * node_count * width * edges
    edge_flops = 2 * edges * width * width * (zero * zero + 4 * one * one + 4 * two * two)
    rows = [zero * width, 2 * one * width, 2 * two * width]
    wide_rows = [pltpu.VMEM((r, edges), BF16) for r in rows]
    values_shape = pltpu.VMEM((zero, width, 5 * edges), BF16)
    products = pltpu.VMEM((zero * width, edges), F32)
    partial_shape = pltpu.VMEM((node_count // 2, features), BF16)
    weights = [pltpu.VMEM(w.shape, BF16) for w in (w_zero, w_one, w_two)]

    prepared = call(
        prepare_kernel,
        (pltpu.VMEM(rotation.shape, F32), edge_block, *weights),
        [rotation, w_zero, w_one, w_two, radial_rows],
        [pltpu.VMEM(rotation.shape, BF16), *weights],
        hbm=4,
        copies=4,
        moved=rotation.size * 8 + edge_flops / edges,
    )
    node_blocks, upstream_blocks, order, prepared = relative_gather(
        nodes[0], cotangent[0], prepared
    )
    wide, scale, *turned = prepared
    x_zero, x_one, x_two, scalar, gate = call(
        functools.partial(nodes_kernel, sizes, order),
        (*wide_rows, edge_block, edge_block),
        [sources, wide, scale, turned[0][:width], w_gate, *node_blocks],
        [*spread, stacked],
        flops=turn_cost,
        moved=4 * sum(rows) * edges,
    )
    gate, *upstream_blocks[:2] = tied(gate, *upstream_blocks[:2])
    m_zero, m_one, m_two, messages = call(
        functools.partial(products_kernel, sizes),
        (*wide_rows, values_shape),
        [x_zero, x_one, x_two, scalar, gate, *turned],
        [products],
        flops=edge_flops,
        moved=6 * sum(rows) * edges,
    )
    g_zero, g_one, g_two, gate_low = call(
        functools.partial(cotangent_kernel, sizes, order),
        (*wide_rows, pltpu.VMEM((width, edges), BF16)),
        [live, targets, wide, scalar, gate, w_gate, m_zero, m_one, m_two]
        + upstream_blocks,
        [*spread, stacked, edge_block, edge_block],
        smem=1,
        flops=turn_cost,
        moved=4 * sum(rows) * edges,
    )

    dp_bits = bits_of("dp")
    stages_a = dp_bits + bits_of("graph")[::-1]
    stages_b = dp_bits[:1] + dp_bits[1:][::-1] + bits_of("graph")
    blocks = lax.axis_size("dp") * lax.axis_size("graph")
    rows_two = 2 * two * two * width
    rows_one = one * one * width
    rows_zero = zero * zero * width
    most = max(rows_two + rows_one, rows_one + rows_zero + width)
    block = -(-most // (16 * blocks)) * 16
    half_list = pltpu.VMEM((blocks * block // 2, width), BF16)
    whole_list = pltpu.VMEM((blocks * block, width), BF16)
    side = zero * width
    square = pltpu.VMEM((side, side), F32)
    a, sent_a = call(
        functools.partial(grad_a_kernel, block, stages_a),
        (half_list, half_list),
        [x_two, g_two, x_one, g_one],
        [whole_list, square],
        flops=edge_flops / 2,
        moved=4 * blocks * block * width,
    )
    b, sent_b = call(
        functools.partial(grad_b_kernel, block, stages_b),
        (half_list, half_list),
        [x_one, g_one, x_zero, g_zero, scalar, gate_low],
        [whole_list, square],
        flops=edge_flops / 2,
        moved=4 * blocks * block * width,
    )

    graph_bits = bits_of("graph")
    last = len(dp_bits) - 1
    for place, (stage_a, stage_b) in enumerate(zip(stages_a, stages_b)):
        if place > 0:
            half = a.shape[0] // 2
            a, sent_a, b, sent_b = a[:half], a[half:], b[:half], b[half:]
        other_a, other_b = exchange(sent_a, *stage_a), exchange(sent_b, *stage_b)
        if place == 0:
            a, b = add_low(a, other_a), add_low(b, other_b)
            b, messages = tied(b, messages)
            sum_kept, sum_sent, grad_kept, grad_sent = call(
                functools.partial(back_kernel, sizes, order),
                (partial_shape,) * 4,
                [
                    live, w_zero, w_one, w_two, sources, targets, wide, scale, messages,
                    g_zero, g_one, g_two,
                ],
                [*weights, *spread, pltpu.VMEM(values_shape.shape, BF16), products],
                smem=1,
                hbm=3,
                copies=3,
                flops=edge_flops + 2 * turn_cost,
                moved=8 * sum(rows) * edges,
            )
            continue
        if place == 1:
            other_a, other_b, sum_kept, sum_sent, grad_kept, grad_sent = tied(
                other_a, other_b, sum_kept, sum_sent, grad_kept, grad_sent
            )
            sum_half = add_low(sum_kept, exchange(sum_sent, *graph_bits[0]))
        if place == last:
            other_a, other_b, sum_half = tied(other_a, other_b, sum_half)
        a, b = add_low(a, other_a), add_low(b, other_b)
    for place in range(len(stages_a))[::-1]:
        half_a = (a, exchange(a, *stages_a[place]))
        half_b = (b, exchange(b, *stages_b[place]))
        if place == last + 2:
            (low_a, high_a), (low_b, high_b) = half_a, half_b
            high_b, grad_kept, grad_sent = tied(high_b, grad_kept, grad_sent)
            half_a, half_b = (low_a, high_a), (low_b, high_b)
            grad_half = add_low(grad_kept, exchange(grad_sent, *graph_bits[0]))
        if place == last:
            (low_a, high_a), (low_b, high_b) = half_a, half_b
            high_a, sum_half, grad_half = tied(high_a, sum_half, grad_half)
            half_a, half_b = (low_a, high_a), (low_b, high_b)
            summed, grad_rows = relative_sum([sum_half, grad_half], graph_bits[1:])
        if place > 0:
            a, b = jnp.concatenate(half_a, axis=0), jnp.concatenate(half_b, axis=0)

    shapes = (
        shaped((2, two * width, two * width), F32),
        shaped((2, one * width, one * width), F32),
        shaped((side, side), F32),
        shaped((width, width), F32),
    )
    half_wide = pltpu.VMEM((blocks * block // 2, width), F32)
    grads = ()
    for high, halves in ((False, (half_a[0], half_b[0])), (True, (half_a[1], half_b[1]))):
        grads = call(
            functools.partial(finish_kernel, sizes, blocks, block, stages_a, stages_b, high),
            shapes,
            [*grads, *halves],
            [half_wide, half_wide],
            hbm=len(grads),
            aliased=len(grads),
            copies=2 * two + 2 * one + zero + 3,
            moved=6 * blocks * block * width,
        )
    grad_two, grad_one, grad_zero, grad_gate = grads
    return (summed[None], grad_rows[None], grad_zero, grad_one, grad_two, grad_gate)


def solution(mesh):
    in_specs = (
        P("dp", "graph", None),
        P("dp", "graph"),
        P("dp", "graph"),
        P("dp", "graph"),
        P("dp", None, None, "graph"),
        P("dp", "graph", None),
        P("dp", "graph", None),
        P(),
        P(),
        P(),
        P(),
    )
    out_specs = (P("dp", "graph", None), P("dp", "graph", None), P(), P(), P(), P())
    return jax.shard_map(
        per_device, mesh=mesh, in_specs=in_specs, out_specs=out_specs, check_vma=False
    )
```
